512 devices in a mesh: mem: 8 (over z_lo), lon: 64 (over z_hi, y, x, core).
Axes of the slice: x: 4, y: 4, z: 16 (z_hi: 2, z_lo: 8; z = z_hi * 8 + z_lo), core: 2. Of those that a mesh axis runs over, the one named last changes fastest.
Arguments:
- latent: bfloat16 [48, 8, 2880, 78], P('mem', None, 'lon'), may hold values from -6 to 6
- conv_weight: bfloat16 [3, 3, 78, 78], replicated, may hold values from -0.21875 to 0.21875
- conv_bias: float32 [78], replicated, may hold values from -3 to 3
- obs_cell: int32 [131072], P('lon'), may hold values from 0 to 28079
- obs_value: float32 [131072], P('lon'), may hold values from -8 to 8
- obs_weight: float32 [131072], P('lon'), may hold values from 0.25 to 4
- obs_list: int32 [8, 2880, 64], P('mem', 'lon'), may hold values from 0 to 6143
Outputs:
- analysis: float32 [48, 8, 2880, 78], P(None, 'mem', 'lon')
The draws below stay inside these ranges and needn't reach their ends.
All inputs are finite; a program needn't handle non-finite values.
Results may differ from the reference program's by a relative error of at most 0.0046.
Values may be sent and summed in bfloat16 or wider, within the bound.
A program may use at most 64 MiB of HBM per device.

```python
import math
import jax
import jax.numpy as jnp
from jax import lax

C = 78
LAT = 8
TLON = 45
NOBS = 2048
OBS_COL = 64
SWEEPS = 6
MEMBERS = 48
NLON = 2880
NOBS_ALL = 131072
N_LON = 64


def set_ends(entries, own_key, low, high):
    extent = entries.shape
    spot = [jax.random.randint(jax.random.fold_in(own_key, axis), (), 0, extent[axis]) for axis in range(len(extent))]
    entries = entries.at[tuple(spot)].set(low)
    longest = extent.index(max(extent))
    spot[longest] = (spot[longest] + 1) % extent[longest]
    return entries.at[tuple(spot)].set(high)


def steps_of(own_key, shape, split, smallest, top_value):
    gain, own = 1.0, jax.random.fold_in(own_key, 6)
    for axis_at, parts in split:
        heights = jnp.exp(jax.random.uniform(jax.random.fold_in(own, axis_at), (parts,), jnp.float32, smallest / len(split), top_value / len(split)))
        gain = gain * jnp.repeat(heights, shape[axis_at] // parts).reshape([-1 if axis == axis_at else 1 for axis in range(len(shape))])
    return gain


def bell_draw(key, shape, deviation, limit, split=(), kind=jnp.bfloat16):
    entries = jax.random.normal(key, shape, jnp.float32) * deviation
    if len(split) > 0:
        entries = steps_of(key, shape, split, -0.22, 0.18) * entries
    return jnp.clip(entries, min=-limit, max=limit).astype(kind)


def setup_inputs(seed: int = 0) -> dict:
    arg_keys = jax.random.split(jax.random.key(seed), 8)
    latent = bell_draw(arg_keys[0], (MEMBERS, LAT, NLON, C), 1.0, 6.0, ((0, 8), (2, 64)))
    conv_weight = bell_draw(arg_keys[1], (3, 3, C, C), (9 * C) ** -0.5, 0.21875)
    conv_bias = bell_draw(arg_keys[2], (C,), 0.5, 3.0, (), jnp.float32)
    obs_cell = set_ends(jax.random.randint(arg_keys[3], (NOBS_ALL,), 0, LAT * TLON * C), jax.random.fold_in(arg_keys[3], 1), 0, (LAT * TLON * C) - 1).astype(jnp.int32)
    obs_value = bell_draw(arg_keys[4], (NOBS_ALL,), 1.5, 8.0, ((0, 64),), jnp.float32)
    obs_weight = jnp.clip(jnp.exp(math.log(4.0) - 2.7725887 * jax.random.uniform(arg_keys[5], (NOBS_ALL,), jnp.float32) ** steps_of(arg_keys[5], (NOBS_ALL,), ((0, 64),), -0.2, 0.2)), 0.25, 4.0)
    obs_list = set_ends(jax.random.randint(arg_keys[6], (LAT, NLON, OBS_COL), 0, 3 * NOBS), jax.random.fold_in(arg_keys[6], 1), 0, (3 * NOBS) - 1).astype(jnp.int32)
    return dict(latent=latent, conv_weight=conv_weight, conv_bias=conv_bias, obs_cell=obs_cell, obs_value=obs_value, obs_weight=obs_weight, obs_list=obs_list)


def analyze(states, ens_obs, values, weights):
    count = states.shape[1]
    hp = lax.Precision.HIGHEST
    ens = ens_obs.astype(jnp.float32)
    ens_mean = lax.optimization_barrier(jnp.mean(ens, axis=1))
    pert = ens - ens_mean[:, None, :]
    depart = values - ens_mean
    eye = jnp.eye(count, dtype=jnp.float32)
    gram = jnp.einsum('bmp,bnp->bmn', pert * weights[:, None, :], pert, precision=hp) + (count - 1.0) * eye
    scale = jnp.trace(gram, axis1=1, axis2=2)
    current = gram / scale[:, None, None]
    inverse = jnp.broadcast_to(eye, gram.shape)
    for repeat in range(SWEEPS):
        factor = 1.5 * eye - 0.5 * jnp.einsum('bmn,bnk->bmk', inverse, current, precision=hp)
        current = jnp.einsum('bmn,bnk->bmk', current, factor, precision=hp)
        inverse = jnp.einsum('bmn,bnk->bmk', factor, inverse, precision=hp)
    root_inv = inverse / jnp.sqrt(scale)[:, None, None]
    project = jnp.einsum('bmp,bp->bm', pert, weights * depart, precision=hp)
    middle = jnp.einsum('bmn,bn->bm', root_inv, project, precision=hp)
    mean_w = jnp.einsum('bmn,bn->bm', root_inv, middle, precision=hp)
    transform = jnp.sqrt(count - 1.0) * root_inv + mean_w[:, :, None]
    field = states.astype(jnp.float32)
    field_mean = lax.optimization_barrier(jnp.mean(field, axis=1))
    field_pert = field - field_mean[:, None, :]
    return field_mean[:, None, :] + jnp.einsum('bjc,bjk->bkc', field_pert, transform, precision=hp)

def reference(latent, conv_weight, conv_bias, obs_cell, obs_value, obs_weight, obs_list):
    members, rows, width, chans = latent.shape

    def decode_member(sample):
        active = jax.nn.silu(sample.astype(jnp.float32)).astype(jnp.bfloat16)
        padded = jnp.pad(active, ((1, 1), (0, 0), (0, 0)))
        wrapped = jnp.concatenate([padded[:, -1:], padded, padded[:, :1]], axis=1)
        total = jnp.zeros((rows, width, chans), jnp.float32)
        for first in range(3):
            for second in range(3):
                piece = wrapped[first:first + rows, second:second + width].reshape(-1, chans)
                total = total + jnp.dot(piece, conv_weight[first, second], preferred_element_type=jnp.float32).reshape(rows, width, chans)
        return (sample.astype(jnp.float32) + total + conv_bias).astype(jnp.bfloat16)
    decoded = lax.map(decode_member, latent)
    tiles = decoded.reshape(members, rows, N_LON, TLON, chans).transpose(2, 0, 1, 3, 4).reshape(N_LON, members, rows * TLON * chans)
    cells = obs_cell.reshape(N_LON, 1, NOBS)
    ens_obs = jnp.take_along_axis(tiles, jnp.broadcast_to(cells, (N_LON, members, NOBS)), axis=2)
    block_ens = jnp.concatenate([jnp.roll(ens_obs, 1, 0), ens_obs, jnp.roll(ens_obs, -1, 0)], axis=2)
    values = obs_value.reshape(N_LON, NOBS)
    weights = obs_weight.reshape(N_LON, NOBS)
    block_val = jnp.concatenate([jnp.roll(values, 1, 0), values, jnp.roll(values, -1, 0)], axis=1)
    block_wgt = jnp.concatenate([jnp.roll(weights, 1, 0), weights, jnp.roll(weights, -1, 0)], axis=1)
    tiled_states = decoded.reshape(members, rows, N_LON, TLON, chans).transpose(2, 1, 3, 0, 4).reshape(N_LON, rows * TLON, members, chans)
    tiled_lists = obs_list.reshape(rows, N_LON, TLON, -1).transpose(1, 0, 2, 3).reshape(N_LON, rows * TLON, -1)

    def per_tile(items):
        states, lists, ens_blk, val_blk, wgt_blk = items
        gathered = jnp.transpose(ens_blk[:, lists], (1, 0, 2))
        return analyze(states, gathered, val_blk[lists], wgt_blk[lists])
    result = lax.map(per_tile, (tiled_states, tiled_lists, block_ens, block_val, block_wgt))
    result = result.reshape(N_LON, rows, TLON, members, chans).transpose(3, 1, 0, 2, 4)
    return result.reshape(members, rows, N_LON * TLON, chans)
```

```python
import functools

import jax
import jax.numpy as jnp
from jax import lax
from jax.experimental import pallas as pl
from jax.experimental.pallas import tpu as pltpu
from jax.sharding import PartitionSpec as P

SWEEPS = 6
MEM = 8
MEMBERS = 48
CHANS = 78
WIDTH = 45
LAT = 8
OWN = 6
PACK = 3
SETS = OWN // PACK
OBS = 2048
OBS_COL = 64
LANES = 128
GROUP = 5
GROUPS = WIDTH // GROUP
CELLS = WIDTH * LAT
BAND = 384
WIDE = 2 * LANES
SLOT = 48
F32 = jnp.float32
BF16 = jnp.bfloat16
MESH = pl.DeviceIdType.MESH


def dot(left, right):
    return jnp.dot(left, right, preferred_element_type=F32)


def silu(v):
    return v / (1.0 + jnp.exp(-v))


def split(v):
    high = v.astype(BF16)
    return high, (v - high.astype(F32)).astype(BF16)


def combine(parts):
    rows = parts.shape[0]
    cube = parts.reshape(rows // LAT, LAT, 3 * WIDE)
    spot = lax.broadcasted_iota(jnp.int32, (rows // LAT, LAT, WIDE), 1)
    above = pltpu.roll(cube[:, :, :WIDE], 1, 1)
    below = pltpu.roll(cube[:, :, 2 * WIDE :], LAT - 1, 1)
    total = cube[:, :, WIDE : 2 * WIDE]
    total = total + jnp.where(spot > 0, above, 0.0) + jnp.where(spot < LAT - 1, below, 0.0)
    return total.reshape(rows, WIDE)


def exchange_kernel(
    lat_ref, w_ref, bias_ref, cell_ref, value_ref, weight_ref,
    blocks, stats, states,
    field, act, wpad, taps, total, halves, turned, cellp, cellc, own, edge_out, edge_in, rows_out,
    edge_sent, edge_got, stat_sent, stat_got, line_sent, sib_sent, outer_sent, block_got,
    state_sent, state_got,
):
    m = lax.axis_index("mem")
    t = lax.axis_index("lon")
    tiles = lax.axis_size("lon")
    core = lax.rem(t, 2)
    left = lax.rem(t + tiles - 1, tiles)
    right = lax.rem(t + 1, tiles)
    outer = jnp.where(core == 0, left, right)
    inner = jnp.where(core == 0, right, left)

    barrier = pltpu.get_barrier_semaphore()
    for lon in (left, right):
        pl.semaphore_signal(barrier, inc=1, device_id={"lon": lon}, device_id_type=MESH)
    for step in range(1, MEM):
        pl.semaphore_signal(
            barrier, inc=1, device_id={"mem": lax.rem(m + step, MEM)}, device_id_type=MESH
        )

    edge_out[...] = jnp.zeros_like(edge_out)
    for side, column in ((0, WIDTH - 1), (1, 0)):
        edge = lat_ref[:, column].astype(F32).reshape(OWN * LAT, CHANS)
        edge_out[side, :, :CHANS] = edge.astype(BF16)
    stats[1, 0] = value_ref[...]
    stats[1, 1] = weight_ref[...]
    pl.semaphore_wait(barrier, MEM + 1)

    edges = [
        pltpu.make_async_remote_copy(
            src_ref=edge_out.at[side],
            dst_ref=edge_in.at[side],
            send_sem=edge_sent.at[side],
            recv_sem=edge_got.at[side],
            device_id={"lon": lon},
            device_id_type=MESH,
        )
        for side, lon in ((0, right), (1, left))
    ]
    stat_copies = [
        pltpu.make_async_remote_copy(
            src_ref=stats.at[1],
            dst_ref=stats.at[2 * side],
            send_sem=stat_sent.at[side],
            recv_sem=stat_got.at[side],
            device_id={"lon": lon},
            device_id_type=MESH,
        )
        for side, lon in ((0, right), (1, left))
    ]
    for copy in edges + stat_copies:
        copy.start()

    wpad[...] = jnp.zeros_like(wpad)
    lane = lax.broadcasted_iota(jnp.int32, (LANES, WIDE), 1)
    depth = lax.broadcasted_iota(jnp.int32, (LANES, WIDE), 0)
    blank = jnp.zeros((LANES, LANES), F32)
    for a in range(3):
        for b in range(3):
            wpad[:CHANS, :CHANS] = w_ref[a, b].astype(F32)
            whole = jnp.concatenate([wpad[...], blank], axis=1)
            for r in range(PACK):
                moved = whole if r == 0 else pltpu.roll(whole, CHANS * r, 1)
                taps[r, b * LANES : (b + 1) * LANES, a * WIDE : (a + 1) * WIDE] = moved.astype(BF16)
    for r in range(PACK):
        same = jnp.where((lane - CHANS * r == depth) & (depth < CHANS), 1.0, 0.0)
        taps[r, 3 * LANES :, :WIDE] = jnp.zeros((LANES, WIDE), BF16)
        taps[r, 3 * LANES :, WIDE : 2 * WIDE] = same.astype(BF16)
        taps[r, 3 * LANES :, 2 * WIDE :] = jnp.zeros((LANES, WIDE), BF16)
    wpad[:1, :CHANS] = bias_ref[...]
    bias = jnp.concatenate([wpad[:8, :], blank[:8, :]], axis=1)
    bias = bias + pltpu.roll(bias, CHANS, 1) + pltpu.roll(bias, 2 * CHANS, 1)
    bias = jnp.where(lane[:8, :] < PACK * CHANS, bias, 0.0)[:1, :]

    flat = cell_ref[...]
    pixel = jnp.floor((flat.astype(F32) + 0.5) * (1.0 / CHANS)).astype(jnp.int32)
    row = jnp.floor((pixel.astype(F32) + 0.5) * (1.0 / WIDTH)).astype(jnp.int32)
    cellc[...] = flat - CHANS * pixel
    cellp[...] = (pixel - WIDTH * row) * LAT + row

    field[...] = jnp.zeros_like(field)
    for k in range(OWN):
        field[k, LAT : LAT + CELLS, :CHANS] = lat_ref[k].astype(F32).reshape(CELLS, CHANS)
    act[...] = silu(field[...])

    span = CELLS + LAT
    for g in range(SETS):
        parts = None
        for r in range(PACK):
            k = PACK * g + r
            sides = [act[k, LAT * b : LAT * b + span, :].astype(BF16) for b in range(3)]
            sides.append(field[k, LAT : LAT + span, :].astype(BF16))
            part = dot(jnp.concatenate(sides, axis=1), taps[r])
            parts = part if parts is None else parts + part
        total[g, :span] = combine(parts) + bias
        total[g, span:] = jnp.zeros((BAND - span, WIDE), F32)

    for side, copy in enumerate(edges):
        copy.wait_recv()
        turn = silu(edge_in[side].astype(F32)).astype(BF16).astype(F32)
        parts = None
        for r in range(PACK):
            pick = [turn[(PACK * g + r) * LAT : (PACK * g + r + 1) * LAT] for g in range(SETS)]
            tap = 2 * side
            part = dot(
                jnp.concatenate(pick, axis=0).astype(BF16), taps[r, tap * LANES : (tap + 1) * LANES]
            )
            parts = part if parts is None else parts + part
        extra = combine(parts)
        first = 0 if side == 0 else CELLS - LAT
        for g in range(SETS):
            total[g, first : first + LAT] += extra[g * LAT : (g + 1) * LAT]

    total[...] = total[...].astype(BF16).astype(F32)
    for g in range(SETS):
        halves[2 * g] = total[g, :, :LANES]
        halves[2 * g + 1] = total[g, :, LANES:]
        turned[g * WIDE : (g + 1) * WIDE] = total[g].T.astype(BF16)

    place = lax.broadcasted_iota(jnp.int32, (BAND, LANES), 0)
    channel = lax.broadcasted_iota(jnp.int32, (WIDE, WIDE), 0)

    def choose(pair, carry):
        first = cellp[pl.ds(2 * pair, 1), :]
        second = cellp[pl.ds(2 * pair + 1, 1), :]
        hot = jnp.concatenate(
            [
                jnp.where(place == first, 1.0, 0.0).astype(BF16),
                jnp.where(place == second, 1.0, 0.0).astype(BF16),
            ],
            axis=1,
        )
        chans = jnp.concatenate(
            [cellc[pl.ds(2 * pair, 1), :], cellc[pl.ds(2 * pair + 1, 1), :]], axis=1
        )
        for g in range(SETS):
            cells = dot(turned[g * WIDE : (g + 1) * WIDE, :], hot)
            for r in range(PACK):
                low, high = CHANS * r // 8 * 8, -(-CHANS * (r + 1) // 8) * 8
                mask = channel[low:high] - CHANS * r == chans
                found = jnp.sum(jnp.where(mask, cells[low:high], 0.0), axis=0, keepdims=True)
                spot = (PACK * g + r) * 16 + 2 * pair
                own[pl.ds(spot, 1), :] = found[:, :LANES]
                own[pl.ds(spot + 1, 1), :] = found[:, LANES:]
        return carry

    lax.fori_loop(0, OBS // WIDE, choose, 0)
    blocks[1, m] = own[...].astype(BF16)

    def hop(slot, kind, way, block, to):
        return pltpu.make_async_remote_copy(
            src_ref=blocks.at[slot, block],
            dst_ref=blocks.at[slot, block],
            send_sem=line_sent.at[kind, way, block],
            recv_sem=block_got.at[slot, block],
            device_id={"mem": to},
            device_id_type=MESH,
        )

    def across(block):
        return pltpu.make_async_remote_copy(
            src_ref=blocks.at[1, block],
            dst_ref=blocks.at[2 * core, block],
            send_sem=sib_sent.at[block],
            recv_sem=block_got.at[2 * core, block],
            device_id={"lon": inner},
            device_id_type=MESH,
        )

    def arrival(slot, block):
        return pltpu.make_async_remote_copy(
            src_ref=blocks.at[1, block],
            dst_ref=blocks.at[slot, block],
            send_sem=outer_sent.at[0],
            recv_sem=block_got.at[slot, block],
            device_id={"lon": inner},
            device_id_type=MESH,
        )

    far = pltpu.make_async_remote_copy(
        src_ref=blocks.at[1, m],
        dst_ref=blocks.at[2 - 2 * core, m],
        send_sem=outer_sent.at[0],
        recv_sem=block_got.at[2 - 2 * core, m],
        device_id={"lon": outer},
        device_id_type=MESH,
    )
    far.start()

    up, down = jnp.minimum(m + 1, MEM - 1), jnp.maximum(m - 1, 0)

    def relay(kind, step):
        slot = 1 if kind == 0 else 2 * core
        low, high = m - step, m + step

        @pl.when(low >= 0)
        def _():
            block = jnp.maximum(low, 0)
            if step > 0 or kind == 1:
                arrival(slot, block).wait_recv()

            @pl.when(m < MEM - 1)
            def _():
                hop(slot, kind, 0, block, up).start()

            if kind == 0:
                across(block).start()

        @pl.when(high < MEM)
        def _():
            block = jnp.minimum(high, MEM - 1)
            if step > 0:
                arrival(slot, block).wait_recv()

            @pl.when(m > 0)
            def _():
                hop(slot, kind, 1, block, down).start()

            if kind == 0 and step > 0:
                across(block).start()

    relay(0, 0)
    for i in range(LAT):
        for g in range(SETS):
            for h in range(2):
                half = 2 * g + h
                rows_out[i, :, half * LANES : (half + 1) * LANES] = halves[
                    half, pl.ds(i, SLOT, stride=LAT), :
                ].astype(BF16)
    states[m] = rows_out[m]
    for step in range(1, MEM + 1):
        if step < MEM:
            relay(0, step)
        relay(1, step - 1)

    def row_copy(to, source):
        return pltpu.make_async_remote_copy(
            src_ref=rows_out.at[to],
            dst_ref=states.at[source],
            send_sem=state_sent.at[to],
            recv_sem=state_got.at[source],
            device_id={"mem": to},
            device_id_type=MESH,
        )

    for step in range(1, MEM):
        row_copy(lax.rem(m + step, MEM), m).start()

    for block in range(MEM):
        arrival(2 - 2 * core, block).wait_recv()
    for copy in stat_copies:
        copy.wait()
    for copy in edges:
        copy.wait_send()
    far.wait_send()
    for block in range(MEM):
        across(block).wait_send()
    for kind in range(2):
        slot = 1 if kind == 0 else 2 * core
        for block in range(MEM):

            @pl.when((m < MEM - 1) & (block <= m))
            def _():
                hop(slot, kind, 0, block, up).wait_send()

            @pl.when((m > 0) & (block >= m))
            def _():
                hop(slot, kind, 1, block, down).wait_send()

    for step in range(1, MEM):
        other = lax.rem(m + step, MEM)
        row_copy(other, other).wait_recv()
        row_copy(other, other).wait_send()


def exchange(lat, weights, bias, cell, value, weight):
    vmem = pl.BlockSpec(memory_space=pltpu.VMEM)
    dma = pltpu.SemaphoreType.DMA
    return pl.pallas_call(
        exchange_kernel,
        out_shape=[
            jax.ShapeDtypeStruct((3, MEM, OWN * 16, LANES), BF16),
            jax.ShapeDtypeStruct((3, 2, 16, LANES), F32),
            jax.ShapeDtypeStruct((MEM, SLOT, SETS * WIDE), BF16),
        ],
        in_specs=[vmem] * 6,
        out_specs=[vmem] * 3,
        scratch_shapes=[
            pltpu.VMEM((OWN, BAND, LANES), F32),
            pltpu.VMEM((OWN, BAND, LANES), F32),
            pltpu.VMEM((LANES, LANES), F32),
            pltpu.VMEM((PACK, 4 * LANES, 3 * WIDE), BF16),
            pltpu.VMEM((SETS, BAND, WIDE), F32),
            pltpu.VMEM((2 * SETS, BAND, LANES), F32),
            pltpu.VMEM((SETS * WIDE, BAND), BF16),
            pltpu.VMEM((16, LANES), jnp.int32),
            pltpu.VMEM((16, LANES), jnp.int32),
            pltpu.VMEM((OWN * 16, LANES), F32),
            pltpu.VMEM((2, OWN * LAT, LANES), BF16),
            pltpu.VMEM((2, OWN * LAT, LANES), BF16),
            pltpu.VMEM((LAT, SLOT, SETS * WIDE), BF16),
            dma((2,)),
            dma((2,)),
            dma((2,)),
            dma((2,)),
            dma((2, 2, MEM)),
            dma((MEM,)),
            dma((1,)),
            dma((3, MEM)),
            dma((MEM,)),
            dma((MEM,)),
        ],
        compiler_params=pltpu.CompilerParams(
            collective_id=0, has_side_effects=True, vmem_limit_bytes=48 * 2**20
        ),
    )(lat, weights, bias, cell, value, weight)


BATCH = 3


def spread(piece):
    return jnp.concatenate([piece] * GROUP + [jnp.zeros((16, WIDE), BF16)], axis=0)


def analysis_kernel(
    list_ref, blocks, stats, states, out, flat, table, picked, columns, diagonal, unpack, done
):
    lane = lax.broadcasted_iota(jnp.int32, (1, WIDE), 1)

    row = lax.broadcasted_iota(jnp.int32, (WIDE, WIDE), 0)
    col = lax.broadcasted_iota(jnp.int32, (WIDE, WIDE), 1)
    mask = jnp.zeros((WIDE, WIDE), F32)
    for s in range(GROUP):
        low, high = s * MEMBERS, (s + 1) * MEMBERS
        mask = jnp.where((row >= low) & (row < high) & (col >= low) & (col < high), 1.0, mask)
    diagonal[...] = mask.astype(BF16)
    row = lax.broadcasted_iota(jnp.int32, (WIDE, LANES), 0)
    col = lax.broadcasted_iota(jnp.int32, (WIDE, LANES), 1)
    for r in range(PACK):
        unpack[:, r * LANES : (r + 1) * LANES] = jnp.where(
            (row - CHANS * r == col) & (col < CHANS), 1.0, 0.0
        ).astype(BF16)

    for s in range(3):
        flat[s * MEM * OWN * 16 : (s + 1) * MEM * OWN * 16] = (
            blocks[s].astype(F32).reshape(MEM * OWN * 16, LANES)
        )
    blank = jnp.zeros((LANES - MEMBERS - 2, LANES), F32)

    def turn(k, carry):
        for s in range(3):
            cells = flat[pl.ds(s * MEM * OWN * 16 + k, MEMBERS, stride=16), :]
            extra = [stats[s, kind, pl.ds(k, 1), :] for kind in range(2)]
            whole = jnp.concatenate([cells] + extra + [blank], axis=0)
            start = pl.multiple_of(s * OBS + k * LANES, LANES)
            table[pl.ds(start, LANES), :] = whole.T
        return carry

    lax.fori_loop(0, 16, turn, 0)

    for source in range(MEM):
        for g in range(SETS):
            parts = dot(states[source, :, g * WIDE : (g + 1) * WIDE], unpack[...])
            for r in range(PACK):
                columns[pl.ds(source * OWN + g * PACK + r, SLOT, stride=MEMBERS), :] = parts[
                    :, r * LANES : (r + 1) * LANES
                ]

    eye = jnp.zeros((MEMBERS, WIDE), F32)
    row48 = lax.broadcasted_iota(jnp.int32, (MEMBERS, WIDE), 0)
    col48 = lax.broadcasted_iota(jnp.int32, (MEMBERS, WIDE), 1)
    for s in range(GROUP):
        eye = jnp.where(col48 - MEMBERS * s == row48, 1.0, eye)

    def block_sum(pieces):
        return dot(jnp.concatenate(pieces, axis=0), diagonal[...])

    def gather(column, carry):
        base = column * OBS_COL
        for o in range(OBS_COL):
            index = list_ref[column, o]
            picked[pl.ds(base + o, 1), :] = table[pl.ds(index, 1), :]
        return carry

    lax.fori_loop(0, WIDTH, gather, 0)

    near = lax.broadcasted_iota(jnp.int32, (OBS_COL, LANES), 1)
    block48 = [(lane >= s * MEMBERS) & (lane < (s + 1) * MEMBERS) for s in range(GROUP)]

    def start(q):
        placed = proj = rate = None
        for s in range(GROUP):
            first = pl.multiple_of((q * GROUP + s) * OBS_COL, OBS_COL)
            rows = picked[pl.ds(first, OBS_COL), :]
            ens = jnp.where(near < MEMBERS, rows, 0.0)
            mean = jnp.sum(ens, axis=1, keepdims=True) * (1.0 / MEMBERS)
            pert = jnp.where(near < MEMBERS, ens - mean, 0.0)
            weight = rows[:, MEMBERS + 1 : MEMBERS + 2]
            scaled = weight * (rows[:, MEMBERS : MEMBERS + 1] - mean)
            wide = jnp.concatenate([pert, jnp.zeros((OBS_COL, LANES), F32)], axis=1)
            if s > 0:
                wide = pltpu.roll(wide, s * MEMBERS, 1)
            part = jnp.sum(wide * scaled, axis=0, keepdims=True)
            spread_weight = jnp.where(block48[s], weight, 0.0)
            placed = wide if placed is None else placed + wide
            proj = part if proj is None else proj + part
            rate = spread_weight if rate is None else rate + spread_weight
        high, low = split(placed)
        scaled_high, scaled_low = split(placed * rate)
        square = lax.dot_general(
            jnp.concatenate([scaled_high, scaled_low, scaled_high], axis=0),
            jnp.concatenate([high, high, low], axis=0),
            (((0,), (0,)), ((), ())),
            preferred_element_type=F32,
        )
        gram = (MEMBERS - 1.0) * eye
        for s in range(GROUP):
            piece = square[s * MEMBERS : (s + 1) * MEMBERS]
            gram = gram + jnp.where(block48[s], piece, 0.0)
        trace = jnp.sum(gram * eye, axis=0, keepdims=True)
        one, rest = split(trace)
        two, three = split(trace - one.astype(F32))
        del rest
        sums = block_sum([one, two, three, jnp.zeros((13, WIDE), BF16)])
        scale = sums[0:1] + sums[1:2] + sums[2:3]
        scale = jnp.where(lane < GROUP * MEMBERS, scale, 1.0)
        return gram / scale, scale, proj

    def times(parts, high, low):
        count = len(parts)
        first = dot(jnp.concatenate([x for pair in parts for x in pair], axis=0), high)
        second = dot(jnp.concatenate([pair[0] for pair in parts], axis=0), low)
        size = parts[0][0].shape[0]
        return [
            first[2 * n * size : (2 * n + 1) * size]
            + first[(2 * n + 1) * size : (2 * n + 2) * size]
            + second[n * size : (n + 1) * size]
            for n in range(count)
        ]

    def lay(pair):
        return [spread(piece) * diagonal[...] for piece in pair]

    def batch(index, carry):
        qs = [index * BATCH + n for n in range(BATCH)]
        state = [start(q) for q in qs]
        ratio = [item[0] for item in state]
        inverse = [None] * BATCH
        for sweep in range(SWEEPS):
            factor = [1.5 * eye - 0.5 * r for r in ratio]
            pairs = [split(f) for f in factor]
            weights = [lay(pair) for pair in pairs]
            for n in range(BATCH):
                todo = []
                if sweep < SWEEPS - 1:
                    todo.append(split(ratio[n]))
                if sweep > 0:
                    todo.append(split(inverse[n]))
                products = times(todo, *weights[n])
                inverse[n] = products[-1] if sweep > 0 else factor[n]
                ratio[n] = products[0]
            if sweep < SWEEPS - 1:
                ratio = [times([split(ratio[n])], *weights[n])[0] for n in range(BATCH)]
        for n in range(BATCH):
            q = qs[n]
            _, scale, proj = state[n]
            root = inverse[n] * lax.rsqrt(scale)
            weights = lay(split(root))
            vector = proj
            for _ in range(2):
                high, low = split(jnp.broadcast_to(vector, (16, WIDE)))
                vector = times([(high, low)], *weights)[0][:1]
            transform = (MEMBERS - 1.0) ** 0.5 * root + vector
            high, low = split(transform)
            sums = block_sum([high, low])
            sums = sums[:MEMBERS] + sums[MEMBERS:]
            transform = transform + (1.0 - sums) * (1.0 / MEMBERS)
            high, low = split(transform)
            first = pl.multiple_of(q * GROUP * MEMBERS, 16)
            field = columns[pl.ds(first, WIDE), :].astype(BF16)
            both = [spread(piece) * diagonal[...] for piece in (high, low)]
            result = dot(both[0], field) + dot(both[1], field)
            for s in range(GROUP):
                piece = result[s * MEMBERS : (s + 1) * MEMBERS]
                done[pl.ds(q * GROUP + s, MEMBERS, stride=WIDTH), :] = piece
        return carry

    lax.fori_loop(0, GROUPS // BATCH, batch, 0)
    out[...] = done[:, :CHANS]


def analysis(lists, blocks, stats, states):
    vmem = pl.BlockSpec(memory_space=pltpu.VMEM)
    return pl.pallas_call(
        analysis_kernel,
        out_shape=jax.ShapeDtypeStruct((MEMBERS * WIDTH, CHANS), F32),
        in_specs=[pl.BlockSpec(memory_space=pltpu.SMEM), vmem, vmem, vmem],
        out_specs=vmem,
        scratch_shapes=[
            pltpu.VMEM((3 * MEM * OWN * 16, LANES), F32),
            pltpu.VMEM((3 * OBS, LANES), F32),
            pltpu.VMEM((WIDTH * OBS_COL, LANES), F32),
            pltpu.VMEM((SLOT * MEMBERS, LANES), F32),
            pltpu.VMEM((WIDE, WIDE), BF16),
            pltpu.VMEM((WIDE, PACK * LANES), BF16),
            pltpu.VMEM((MEMBERS * WIDTH, LANES), F32),
        ],
        compiler_params=pltpu.CompilerParams(vmem_limit_bytes=48 * 2**20),
    )(lists, blocks, stats, states)


def local(latent, conv_weight, conv_bias, obs_cell, obs_value, obs_weight, obs_list):
    blocks, stats, states = exchange(
        jnp.transpose(latent, (0, 2, 1, 3)),
        conv_weight,
        conv_bias.reshape(1, CHANS),
        obs_cell.reshape(16, LANES),
        obs_value.reshape(16, LANES),
        obs_weight.reshape(16, LANES),
    )
    result = analysis(obs_list.reshape(WIDTH, OBS_COL), blocks, stats, states)
    return jnp.transpose(result.reshape(MEMBERS, WIDTH, 1, CHANS), (0, 2, 1, 3))


def solution(mesh):
    placed = (
        P("mem", None, "lon", None),
        P(),
        P(),
        P("lon"),
        P("lon"),
        P("lon"),
        P("mem", "lon", None),
    )
    return jax.shard_map(
        local, mesh=mesh, in_specs=placed, out_specs=P(None, "mem", "lon", None), check_vma=False
    )
```

```python
import functools

import jax
import jax.numpy as jnp
from jax import lax
from jax.experimental import pallas as pl
from jax.experimental.pallas import tpu as pltpu
from jax.sharding import PartitionSpec as P

SWEEPS = 6
MEM = 8
MEMBERS = 48
CHANS = 78
WIDTH = 45
LAT = 8
OWN = 6
PACK = 3
SETS = OWN // PACK
OBS = 2048
OBS_COL = 64
LANES = 128
GROUP = 5
GROUPS = WIDTH // GROUP
CELLS = WIDTH * LAT
BAND = 384
WIDE = 2 * LANES
SLOT = 48
F32 = jnp.float32
BF16 = jnp.bfloat16
MESH = pl.DeviceIdType.MESH


def dot(left, right):
    return jnp.dot(left, right, preferred_element_type=F32)


def silu(v):
    return v / (1.0 + jnp.exp(-v))


def split(v):
    high = v.astype(BF16)
    return high, (v - high.astype(F32)).astype(BF16)


def combine(parts):
    rows = parts.shape[0]
    cube = parts.reshape(rows // LAT, LAT, 3 * WIDE)
    spot = lax.broadcasted_iota(jnp.int32, (rows // LAT, LAT, WIDE), 1)
    above = pltpu.roll(cube[:, :, :WIDE], 1, 1)
    below = pltpu.roll(cube[:, :, 2 * WIDE :], LAT - 1, 1)
    total = cube[:, :, WIDE : 2 * WIDE]
    total = total + jnp.where(spot > 0, above, 0.0) + jnp.where(spot < LAT - 1, below, 0.0)
    return total.reshape(rows, WIDE)


def exchange_kernel(
    lat_hbm, w_hbm, bias_hbm, cell_hbm, value_hbm, weight_hbm,
    blocks, stats, states, edges,
    lat_ref, w_ref, bias_ref, cell_ref, field, act, wpad, taps, total, halves, turned, cellp, cellc,
    own, edge_out, edge_in, rows_out, ends, ends_out,
    loaded, edge_sent, edge_got, stat_sent, stat_got, mate_sent, sib_sent, outer_sent, block_got,
    state_sent, state_got, end_sent, end_got,
):
    m = lax.axis_index("mem")
    t = lax.axis_index("lon")
    tiles = lax.axis_size("lon")
    core = lax.rem(t, 2)
    left = lax.rem(t + tiles - 1, tiles)
    right = lax.rem(t + 1, tiles)
    outer = jnp.where(core == 0, left, right)
    inner = jnp.where(core == 0, right, left)
    mine, theirs = 2 * core, 2 - 2 * core
    far = lax.rem(jnp.where(core == 0, t, t + 1), tiles // 2) == 0

    barrier = pltpu.get_barrier_semaphore()
    for lon in (left, right):
        pl.semaphore_signal(barrier, inc=1, device_id={"lon": lon}, device_id_type=MESH)

    @pl.when(far)
    def _():
        for step in range(1, MEM):
            to = {"mem": lax.rem(m + step, MEM), "lon": outer}
            pl.semaphore_signal(barrier, inc=1, device_id=to, device_id_type=MESH)

    for step in range(1, MEM):
        to = {"mem": lax.rem(m + step, MEM)}
        pl.semaphore_signal(barrier, inc=1, device_id=to, device_id_type=MESH)

    loads = [
        pltpu.make_async_copy(source, target, loaded.at[n])
        for n, (source, target) in enumerate(
            (
                (lat_hbm, lat_ref),
                (w_hbm, w_ref),
                (bias_hbm, bias_ref),
                (cell_hbm, cell_ref),
                (value_hbm, stats.at[1, 0]),
                (weight_hbm, stats.at[1, 1]),
            )
        )
    ]
    for load in loads:
        load.start()

    edge_out[...] = jnp.zeros_like(edge_out)
    field[...] = jnp.zeros_like(field)
    wpad[...] = jnp.zeros_like(wpad)
    ends[...] = jnp.zeros_like(ends)
    for load in loads:
        load.wait()
    for side, column in ((0, WIDTH - 1), (1, 0)):
        edge = lat_ref[:, column].astype(F32).reshape(OWN * LAT, CHANS)
        edge_out[side, :, :CHANS] = edge.astype(BF16)

    lane = lax.broadcasted_iota(jnp.int32, (LANES, WIDE), 1)
    depth = lax.broadcasted_iota(jnp.int32, (LANES, WIDE), 0)
    blank = jnp.zeros((LANES, LANES), F32)
    for a in range(3):
        for b in range(3):
            wpad[:CHANS, :CHANS] = w_ref[a, b].astype(F32)
            whole = jnp.concatenate([wpad[...], blank], axis=1)
            for r in range(PACK):
                moved = whole if r == 0 else pltpu.roll(whole, CHANS * r, 1)
                taps[r, b * LANES : (b + 1) * LANES, a * WIDE : (a + 1) * WIDE] = moved.astype(BF16)
    for r in range(PACK):
        same = jnp.where((lane - CHANS * r == depth) & (depth < CHANS), 1.0, 0.0)
        taps[r, 3 * LANES :, :WIDE] = jnp.zeros((LANES, WIDE), BF16)
        taps[r, 3 * LANES :, WIDE : 2 * WIDE] = same.astype(BF16)
        taps[r, 3 * LANES :, 2 * WIDE :] = jnp.zeros((LANES, WIDE), BF16)
    wpad[:1, :CHANS] = bias_ref[...]
    bias = jnp.concatenate([wpad[:8, :], blank[:8, :]], axis=1)
    bias = bias + pltpu.roll(bias, CHANS, 1) + pltpu.roll(bias, 2 * CHANS, 1)
    bias = jnp.where(lane[:8, :] < PACK * CHANS, bias, 0.0)[:1, :]

    flat = cell_ref[...]
    pixel = jnp.floor((flat.astype(F32) + 0.5) * (1.0 / CHANS)).astype(jnp.int32)
    row = jnp.floor((pixel.astype(F32) + 0.5) * (1.0 / WIDTH)).astype(jnp.int32)
    cellc[...] = flat - CHANS * pixel
    cellp[...] = (pixel - WIDTH * row) * LAT + row

    pl.semaphore_wait(barrier, jnp.where(far, 2 * MEM, MEM + 1))

    edge_copies = [
        pltpu.make_async_remote_copy(
            src_ref=edge_out.at[side],
            dst_ref=edge_in.at[side],
            send_sem=edge_sent.at[side],
            recv_sem=edge_got.at[side],
            device_id={"lon": lon},
            device_id_type=MESH,
        )
        for side, lon in ((0, right), (1, left))
    ]
    stat_copies = [
        pltpu.make_async_remote_copy(
            src_ref=stats.at[1],
            dst_ref=stats.at[2 * side],
            send_sem=stat_sent.at[side],
            recv_sem=stat_got.at[side],
            device_id={"lon": lon},
            device_id_type=MESH,
        )
        for side, lon in ((0, right), (1, left))
    ]
    for copy in edge_copies + stat_copies:
        copy.start()

    for k in range(OWN):
        field[k, LAT : LAT + CELLS, :CHANS] = lat_ref[k].astype(F32).reshape(CELLS, CHANS)
    act[...] = silu(field[...])

    span = CELLS + LAT
    for g in range(SETS):
        parts = None
        for r in range(PACK):
            k = PACK * g + r
            sides = [act[k, LAT * b : LAT * b + span, :].astype(BF16) for b in range(3)]
            sides.append(field[k, LAT : LAT + span, :].astype(BF16))
            part = dot(jnp.concatenate(sides, axis=1), taps[r])
            parts = part if parts is None else parts + part
        summed = combine(parts) + bias
        total[g, :span] = summed
        total[g, span:] = jnp.zeros((BAND - span, WIDE), F32)
        for h in range(2):
            halves[2 * g + h] = total[g, :, h * LANES : (h + 1) * LANES]

    for i in range(LAT):
        for half in range(2 * SETS):
            rows_out[i, :, half * LANES : (half + 1) * LANES] = halves[
                half, pl.ds(i, SLOT, stride=LAT), :
            ].astype(BF16)
    states[m] = rows_out[m]

    def row_copy(to, source):
        return pltpu.make_async_remote_copy(
            src_ref=rows_out.at[to],
            dst_ref=states.at[source],
            send_sem=state_sent.at[to],
            recv_sem=state_got.at[source],
            device_id={"mem": to},
            device_id_type=MESH,
        )

    def end_copy(to, source):
        return pltpu.make_async_remote_copy(
            src_ref=ends_out.at[to],
            dst_ref=edges.at[source],
            send_sem=end_sent.at[to],
            recv_sem=end_got.at[source],
            device_id={"mem": to},
            device_id_type=MESH,
        )

    for step in range(1, MEM):
        row_copy(lax.rem(m + step, MEM), m).start()

    for side, copy in enumerate(edge_copies):
        copy.wait_recv()
        turn = silu(edge_in[side].astype(F32)).astype(BF16).astype(F32)
        parts = None
        for r in range(PACK):
            pick = [turn[(PACK * g + r) * LAT : (PACK * g + r + 1) * LAT] for g in range(SETS)]
            tap = 2 * side
            part = dot(
                jnp.concatenate(pick, axis=0).astype(BF16), taps[r, tap * LANES : (tap + 1) * LANES]
            )
            parts = part if parts is None else parts + part
        extra = combine(parts)
        first = 0 if side == 0 else CELLS - LAT
        for g in range(SETS):
            total[g, first : first + LAT] += extra[g * LAT : (g + 1) * LAT]
            for h in range(2):
                ends[pl.ds(4 * g + 2 * h + side, LAT, stride=16), :] = total[
                    g, first : first + LAT, h * LANES : (h + 1) * LANES
                ]
    ends_out[...] = ends[...].astype(BF16).reshape(LAT, 16, LANES)
    edges[m] = ends_out[m]
    for g in range(SETS):
        turned[g * WIDE : (g + 1) * WIDE] = total[g].T.astype(BF16)

    place = lax.broadcasted_iota(jnp.int32, (BAND, LANES), 0)
    channel = lax.broadcasted_iota(jnp.int32, (WIDE, WIDE), 0)

    def choose(pair, carry):
        first = cellp[pl.ds(2 * pair, 1), :]
        second = cellp[pl.ds(2 * pair + 1, 1), :]
        hot = jnp.concatenate(
            [
                jnp.where(place == first, 1.0, 0.0).astype(BF16),
                jnp.where(place == second, 1.0, 0.0).astype(BF16),
            ],
            axis=1,
        )
        chans = jnp.concatenate(
            [cellc[pl.ds(2 * pair, 1), :], cellc[pl.ds(2 * pair + 1, 1), :]], axis=1
        )
        for g in range(SETS):
            cells = dot(turned[g * WIDE : (g + 1) * WIDE, :], hot)
            for r in range(PACK):
                low, high = CHANS * r // 8 * 8, -(-CHANS * (r + 1) // 8) * 8
                mask = channel[low:high] - CHANS * r == chans
                found = jnp.sum(jnp.where(mask, cells[low:high], 0.0), axis=0, keepdims=True)
                spot = (PACK * g + r) * 16 + 2 * pair
                own[pl.ds(spot, 1), :] = found[:, :LANES]
                own[pl.ds(spot + 1, 1), :] = found[:, LANES:]
        return carry

    lax.fori_loop(0, OBS // WIDE, choose, 0)
    blocks[1, m] = own[...].astype(BF16)

    def arrival(slot, block):
        return pltpu.make_async_remote_copy(
            src_ref=blocks.at[1, block],
            dst_ref=blocks.at[slot, block],
            send_sem=sib_sent.at[block],
            recv_sem=block_got.at[slot, block],
            device_id={"lon": inner},
            device_id_type=MESH,
        )

    def along(block, sent, to):
        return pltpu.make_async_remote_copy(
            src_ref=blocks.at[1, block],
            dst_ref=blocks.at[1, block],
            send_sem=mate_sent.at[sent],
            recv_sem=block_got.at[1, block],
            device_id={"mem": to},
            device_id_type=MESH,
        )

    def across(block):
        return pltpu.make_async_remote_copy(
            src_ref=blocks.at[1, block],
            dst_ref=blocks.at[mine, block],
            send_sem=sib_sent.at[block],
            recv_sem=block_got.at[mine, block],
            device_id={"lon": inner},
            device_id_type=MESH,
        )

    def outward(block, sent, to):
        return pltpu.make_async_remote_copy(
            src_ref=blocks.at[1, block],
            dst_ref=blocks.at[theirs, block],
            send_sem=outer_sent.at[sent],
            recv_sem=block_got.at[theirs, block],
            device_id={"mem": to, "lon": outer},
            device_id_type=MESH,
        )

    half = m // 4 * 4
    partner = lax.rem(m + 4, MEM)
    partner_half = 4 - half
    mates = [half + lax.rem(m + step, 4) for step in range(1, 4)]
    partner_mates = [partner_half + lax.rem(m + step, 4) for step in range(1, 4)]

    @pl.when(far)
    def _():
        for step in range(MEM):
            to = lax.rem(m + step, MEM)
            outward(m, to, to).start()

    def pass_on(block):
        across(block).start()

        @pl.when(jnp.logical_not(far))
        def _():
            outward(block, block, m).start()

    along(m, 3, partner).start()
    for n in range(3):
        along(m, n, mates[n]).start()
    pass_on(m)
    for step in range(1, MEM):
        end_copy(lax.rem(m + step, MEM), m).start()
    for n in range(3):
        arrival(1, mates[n]).wait_recv()
        pass_on(mates[n])
    arrival(1, partner).wait_recv()
    for n in range(3):
        along(partner, 4 + n, mates[n]).start()
    pass_on(partner)
    for n in range(3):
        arrival(1, partner_mates[n]).wait_recv()
        pass_on(partner_mates[n])

    for block in range(MEM):
        arrival(mine, block).wait_recv()
        arrival(theirs, block).wait_recv()
    for copy in stat_copies:
        copy.wait()
    for copy in edge_copies:
        copy.wait_send()
    for block in range(MEM):
        across(block).wait_send()
        outward(block, block, m).wait_send()
    along(m, 3, partner).wait_send()
    for n in range(3):
        along(m, n, mates[n]).wait_send()
        along(partner, 4 + n, mates[n]).wait_send()
    for step in range(1, MEM):
        other = lax.rem(m + step, MEM)
        row_copy(other, other).wait_recv()
        row_copy(other, other).wait_send()
        end_copy(other, other).wait_recv()
        end_copy(other, other).wait_send()


def exchange(lat, weights, bias, cell, value, weight):
    vmem = pl.BlockSpec(memory_space=pltpu.VMEM)
    hbm = pl.BlockSpec(memory_space=pltpu.HBM)
    dma = pltpu.SemaphoreType.DMA
    return pl.pallas_call(
        exchange_kernel,
        out_shape=[
            jax.ShapeDtypeStruct((3, MEM, OWN * 16, LANES), BF16),
            jax.ShapeDtypeStruct((3, 2, 16, LANES), F32),
            jax.ShapeDtypeStruct((MEM, SLOT, SETS * WIDE), BF16),
            jax.ShapeDtypeStruct((MEM, 16, LANES), BF16),
        ],
        in_specs=[hbm] * 6,
        out_specs=[vmem] * 4,
        scratch_shapes=[
            pltpu.VMEM(lat.shape, BF16),
            pltpu.VMEM(weights.shape, BF16),
            pltpu.VMEM(bias.shape, F32),
            pltpu.VMEM(cell.shape, jnp.int32),
            pltpu.VMEM((OWN, BAND, LANES), F32),
            pltpu.VMEM((OWN, BAND, LANES), F32),
            pltpu.VMEM((LANES, LANES), F32),
            pltpu.VMEM((PACK, 4 * LANES, 3 * WIDE), BF16),
            pltpu.VMEM((SETS, BAND, WIDE), F32),
            pltpu.VMEM((2 * SETS, BAND, LANES), F32),
            pltpu.VMEM((SETS * WIDE, BAND), BF16),
            pltpu.VMEM((16, LANES), jnp.int32),
            pltpu.VMEM((16, LANES), jnp.int32),
            pltpu.VMEM((OWN * 16, LANES), F32),
            pltpu.VMEM((2, OWN * LAT, LANES), BF16),
            pltpu.VMEM((2, OWN * LAT, LANES), BF16),
            pltpu.VMEM((LAT, SLOT, SETS * WIDE), BF16),
            pltpu.VMEM((LAT * 16, LANES), F32),
            pltpu.VMEM((LAT, 16, LANES), BF16),
            dma((6,)),
            dma((2,)),
            dma((2,)),
            dma((2,)),
            dma((2,)),
            dma((7,)),
            dma((MEM,)),
            dma((MEM,)),
            dma((3, MEM)),
            dma((MEM,)),
            dma((MEM,)),
            dma((MEM,)),
            dma((MEM,)),
        ],
        compiler_params=pltpu.CompilerParams(
            collective_id=0, has_side_effects=True, vmem_limit_bytes=48 * 2**20
        ),
    )(lat, weights, bias, cell, value, weight)


def spread(piece):
    return jnp.concatenate([piece] * GROUP + [jnp.zeros((16, WIDE), BF16)], axis=0)


def analysis_kernel(
    list_ref, blocks, stats, states, edges, out,
    flat, table, picked, placing, stage, columns, diagonal, unpack, done,
):
    row = lax.broadcasted_iota(jnp.int32, (WIDE, WIDE), 0)
    col = lax.broadcasted_iota(jnp.int32, (WIDE, WIDE), 1)
    mask = jnp.zeros((WIDE, WIDE), F32)
    for s in range(GROUP):
        low, high = s * MEMBERS, (s + 1) * MEMBERS
        mask = jnp.where((row >= low) & (row < high) & (col >= low) & (col < high), 1.0, mask)
    diagonal[...] = mask.astype(BF16)
    row = lax.broadcasted_iota(jnp.int32, (WIDE, LANES), 0)
    col = lax.broadcasted_iota(jnp.int32, (WIDE, LANES), 1)
    for r in range(PACK):
        unpack[:, r * LANES : (r + 1) * LANES] = jnp.where(
            (row - CHANS * r == col) & (col < CHANS), 1.0, 0.0
        ).astype(BF16)
    row = lax.broadcasted_iota(jnp.int32, (LANES, WIDE), 0)
    col = lax.broadcasted_iota(jnp.int32, (LANES, WIDE), 1)
    member = row < MEMBERS
    for s in range(GROUP):
        inside = (col >= s * MEMBERS) & (col < (s + 1) * MEMBERS)
        kinds = (
            member & (col - s * MEMBERS == row),
            member & inside,
            ((row == MEMBERS) | (row == MEMBERS + 2)) & inside,
            ((row == MEMBERS + 1) | (row == MEMBERS + 3)) & inside,
        )
        for n, kind in enumerate(kinds):
            placing[s * LANES : (s + 1) * LANES, n * WIDE : (n + 1) * WIDE] = jnp.where(
                kind, 1.0, 0.0
            ).astype(BF16)

    for s in range(3):
        flat[s * MEM * OWN * 16 : (s + 1) * MEM * OWN * 16] = (
            blocks[s].astype(F32).reshape(MEM * OWN * 16, LANES)
        )
    blank = jnp.zeros((LANES - MEMBERS - 4, LANES), F32)

    def turn(k, carry):
        for s in range(3):
            cells = flat[pl.ds(s * MEM * OWN * 16 + k, MEMBERS, stride=16), :]
            extra = [stats[s, kind, pl.ds(k, 1), :] for kind in range(2)]
            high = [v.astype(BF16).astype(F32) for v in extra]
            low = [v - h for v, h in zip(extra, high)]
            whole = jnp.concatenate([cells] + high + low + [blank], axis=0)
            start = pl.multiple_of(s * OBS + k * LANES, LANES)
            table[pl.ds(start, LANES), :] = whole.T
        return carry

    lax.fori_loop(0, 16, turn, 0)

    for source in range(MEM):
        for g in range(SETS):
            parts = dot(states[source, :, g * WIDE : (g + 1) * WIDE], unpack[...])
            for r in range(PACK):
                columns[pl.ds(source * OWN + g * PACK + r, SLOT, stride=MEMBERS), :] = parts[
                    :, r * LANES : (r + 1) * LANES
                ]
    ends = edges[...].astype(F32)
    for g in range(SETS):
        sides = [
            jnp.concatenate([ends[:, 4 * g + side, :], ends[:, 4 * g + 2 + side, :]], axis=1)
            for side in range(2)
        ]
        parts = dot(jnp.concatenate(sides, axis=0).astype(BF16), unpack[...])
        for side, column in ((0, 0), (1, WIDTH - 1)):
            for r in range(PACK):
                columns[pl.ds(column * MEMBERS + g * PACK + r, MEM, stride=OWN), :] = parts[
                    side * MEM : (side + 1) * MEM, r * LANES : (r + 1) * LANES
                ]

    def gather(q, carry):
        base = q * OBS_COL
        for s in range(GROUP):
            for o in range(OBS_COL):
                index = list_ref[q * GROUP + s, 0, o]
                picked[s, pl.ds(base + o, 1), :] = table[pl.ds(index, 1), :]
        return carry

    lax.fori_loop(0, GROUPS, gather, 0)
    found = jnp.concatenate([picked[s].astype(BF16) for s in range(GROUP)], axis=1)
    stage[...] = dot(found, placing[...])

    eye = jnp.zeros((MEMBERS, WIDE), F32)
    row48 = lax.broadcasted_iota(jnp.int32, (MEMBERS, WIDE), 0)
    col48 = lax.broadcasted_iota(jnp.int32, (MEMBERS, WIDE), 1)
    for s in range(GROUP):
        eye = jnp.where(col48 - MEMBERS * s == row48, 1.0, eye)
    lane = lax.broadcasted_iota(jnp.int32, (1, WIDE), 1)
    block48 = [(lane >= s * MEMBERS) & (lane < (s + 1) * MEMBERS) for s in range(GROUP)]
    every = range(GROUPS)

    def block_sum(pieces):
        return dot(jnp.concatenate(pieces, axis=0), diagonal[...])

    grams, proj, traces = [], [], []
    for q in every:
        rows = slice(q * OBS_COL, (q + 1) * OBS_COL)
        mean = stage[rows, WIDE : 2 * WIDE] * (1.0 / MEMBERS)
        pert = stage[rows, :WIDE] - mean
        depart = stage[rows, 2 * WIDE : 3 * WIDE] - mean
        scaled = pert * stage[rows, 3 * WIDE :]
        proj.append(jnp.sum(scaled * depart, axis=0, keepdims=True))
        traces.append(jnp.sum(scaled * pert, axis=0, keepdims=True))
        high, low = split(pert)
        scaled_high, scaled_low = split(scaled)
        square = lax.dot_general(
            jnp.concatenate([scaled_high, scaled_low, scaled_high], axis=0),
            jnp.concatenate([high, high, low], axis=0),
            (((0,), (0,)), ((), ())),
            preferred_element_type=F32,
        )
        gram = (MEMBERS - 1.0) * eye
        for s in range(GROUP):
            piece = square[s * MEMBERS : (s + 1) * MEMBERS]
            gram = gram + jnp.where(block48[s], piece, 0.0)
        grams.append(gram)
    trace = jnp.concatenate(traces + [jnp.zeros((16 - GROUPS, WIDE), F32)], axis=0)
    one = trace.astype(BF16)
    two, three = split(trace - one.astype(F32))
    sums = block_sum([one, two, three])
    scales = MEMBERS * (MEMBERS - 1.0) + sums[:16] + sums[16:32] + sums[32:]
    invert, reroot = 1.0 / scales, lax.rsqrt(scales)

    def times(parts, high, low):
        count = len(parts)
        first = dot(jnp.concatenate([x for pair in parts for x in pair], axis=0), high)
        second = dot(jnp.concatenate([pair[0] for pair in parts], axis=0), low)
        size = parts[0][0].shape[0]
        return [
            first[2 * n * size : (2 * n + 1) * size]
            + first[(2 * n + 1) * size : (2 * n + 2) * size]
            + second[n * size : (n + 1) * size]
            for n in range(count)
        ]

    def lay(pair):
        return [spread(piece) * diagonal[...] for piece in pair]

    ratio = [grams[q] * invert[q : q + 1] for q in every]
    inverse = [None] * GROUPS
    for sweep in range(SWEEPS):
        factor = [1.5 * eye - 0.5 * r for r in ratio]
        weights = [lay(split(f)) for f in factor]
        products = []
        for q in every:
            todo = []
            if sweep < SWEEPS - 1:
                todo.append(split(ratio[q]))
            if sweep > 0:
                todo.append(split(inverse[q]))
            products.append(times(todo, *weights[q]))
        inverse = [products[q][-1] if sweep > 0 else factor[q] for q in every]
        if sweep < SWEEPS - 1:
            ratio = [times([split(products[q][0])], *weights[q])[0] for q in every]

    root = [inverse[q] * reroot[q : q + 1] for q in every]
    weights = [lay(split(r)) for r in root]
    vector = proj
    spot = lax.broadcasted_iota(jnp.int32, (16, WIDE), 0)
    for _ in range(2):
        rows = []
        for q in every:
            high = vector[q].astype(BF16).astype(F32)
            low = vector[q] - high
            rows.append(jnp.where(spot == 0, high, jnp.where(spot == 1, low, 0.0)).astype(BF16))
        first = [dot(rows[q], weights[q][0]) for q in every]
        second = [dot(rows[q], weights[q][1]) for q in every]
        vector = [first[q][0:1] + first[q][1:2] + second[q][0:1] for q in every]
    transform = [(MEMBERS - 1.0) ** 0.5 * root[q] + vector[q] for q in every]
    sums = block_sum([piece for t in transform for piece in split(t)])
    pieces = []
    for q in every:
        at = 2 * q * MEMBERS
        both = sums[at : at + MEMBERS] + sums[at + MEMBERS : at + 2 * MEMBERS]
        pieces.append(lay(split(transform[q] + (1.0 - both) * (1.0 / MEMBERS))))
    for q in every:
        field = columns[q * GROUP * MEMBERS : q * GROUP * MEMBERS + WIDE, :].astype(BF16)
        result = dot(pieces[q][0], field) + dot(pieces[q][1], field)
        for s in range(GROUP):
            done[pl.ds(q * GROUP + s, MEMBERS, stride=WIDTH), :] = result[
                s * MEMBERS : (s + 1) * MEMBERS
            ]
    out[...] = done[:, :CHANS]


def analysis(lists, blocks, stats, states, edges):
    vmem = pl.BlockSpec(memory_space=pltpu.VMEM)
    return pl.pallas_call(
        analysis_kernel,
        out_shape=jax.ShapeDtypeStruct((MEMBERS * WIDTH, CHANS), F32),
        in_specs=[pl.BlockSpec(memory_space=pltpu.SMEM)] + [vmem] * 4,
        out_specs=vmem,
        scratch_shapes=[
            pltpu.VMEM((3 * MEM * OWN * 16, LANES), F32),
            pltpu.VMEM((3 * OBS, LANES), F32),
            pltpu.VMEM((GROUP, GROUPS * OBS_COL, LANES), F32),
            pltpu.VMEM((GROUP * LANES, 4 * WIDE), BF16),
            pltpu.VMEM((GROUPS * OBS_COL, 4 * WIDE), F32),
            pltpu.VMEM((SLOT * MEMBERS, LANES), F32),
            pltpu.VMEM((WIDE, WIDE), BF16),
            pltpu.VMEM((WIDE, PACK * LANES), BF16),
            pltpu.VMEM((MEMBERS * WIDTH, LANES), F32),
        ],
        compiler_params=pltpu.CompilerParams(vmem_limit_bytes=48 * 2**20),
    )(lists, blocks, stats, states, edges)


def local(latent, conv_weight, conv_bias, obs_cell, obs_value, obs_weight, obs_list):
    blocks, stats, states, edges = exchange(
        jnp.transpose(latent, (0, 2, 1, 3)),
        conv_weight,
        conv_bias.reshape(1, CHANS),
        obs_cell.reshape(16, LANES),
        obs_value.reshape(16, LANES),
        obs_weight.reshape(16, LANES),
    )
    result = analysis(obs_list.reshape(WIDTH, 1, OBS_COL), blocks, stats, states, edges)
    return jnp.transpose(result.reshape(MEMBERS, WIDTH, 1, CHANS), (0, 2, 1, 3))


def solution(mesh):
    placed = (
        P("mem", None, "lon", None),
        P(),
        P(),
        P("lon"),
        P("lon"),
        P("lon"),
        P("mem", "lon", None),
    )
    return jax.shard_map(
        local, mesh=mesh, in_specs=placed, out_specs=P(None, "mem", "lon", None), check_vma=False
    )
```

```python
import functools

import jax
import jax.numpy as jnp
from jax import lax
from jax.experimental import pallas as pl
from jax.experimental.pallas import tpu as pltpu
from jax.sharding import PartitionSpec as P

SWEEPS = 6
MEM = 8
MEMBERS = 48
CHANS = 78
WIDTH = 45
LAT = 8
OWN = 6
PACK = 3
SETS = OWN // PACK
OBS = 2048
OBS_COL = 64
LANES = 128
GROUP = 5
GROUPS = WIDTH // GROUP
CELLS = WIDTH * LAT
BAND = 384
WIDE = 2 * LANES
SLOT = 48
F32 = jnp.float32
BF16 = jnp.bfloat16
MESH = pl.DeviceIdType.MESH


def dot(left, right):
    return jnp.dot(left, right, preferred_element_type=F32)


def silu(v):
    return v / (1.0 + jnp.exp(-v))


def split(v):
    high = v.astype(BF16)
    return high, (v - high.astype(F32)).astype(BF16)


def combine(parts):
    rows = parts.shape[0]
    cube = parts.reshape(rows // LAT, LAT, 3 * WIDE)
    spot = lax.broadcasted_iota(jnp.int32, (rows // LAT, LAT, WIDE), 1)
    above = pltpu.roll(cube[:, :, :WIDE], 1, 1)
    below = pltpu.roll(cube[:, :, 2 * WIDE :], LAT - 1, 1)
    total = cube[:, :, WIDE : 2 * WIDE]
    total = total + jnp.where(spot > 0, above, 0.0) + jnp.where(spot < LAT - 1, below, 0.0)
    return total.reshape(rows, WIDE)


def spread(piece):
    return jnp.concatenate([piece] * GROUP + [jnp.zeros((16, WIDE), BF16)], axis=0)


def build_constants(placing, diagonal, unpack):
    row = lax.broadcasted_iota(jnp.int32, (WIDE, WIDE), 0)
    col = lax.broadcasted_iota(jnp.int32, (WIDE, WIDE), 1)
    mask = jnp.zeros((WIDE, WIDE), F32)
    for s in range(GROUP):
        low, high = s * MEMBERS, (s + 1) * MEMBERS
        mask = jnp.where((row >= low) & (row < high) & (col >= low) & (col < high), 1.0, mask)
    diagonal[...] = mask.astype(BF16)
    row = lax.broadcasted_iota(jnp.int32, (WIDE, LANES), 0)
    col = lax.broadcasted_iota(jnp.int32, (WIDE, LANES), 1)
    for r in range(PACK):
        unpack[:, r * LANES : (r + 1) * LANES] = jnp.where(
            (row - CHANS * r == col) & (col < CHANS), 1.0, 0.0
        ).astype(BF16)
    row = lax.broadcasted_iota(jnp.int32, (LANES, WIDE), 0)
    col = lax.broadcasted_iota(jnp.int32, (LANES, WIDE), 1)
    member = row < MEMBERS
    for s in range(GROUP):
        inside = (col >= s * MEMBERS) & (col < (s + 1) * MEMBERS)
        kinds = (
            member & (col - s * MEMBERS == row),
            member & inside,
            ((row == MEMBERS) | (row == MEMBERS + 2)) & inside,
            ((row == MEMBERS + 1) | (row == MEMBERS + 3)) & inside,
        )
        for n, kind in enumerate(kinds):
            placing[s * LANES : (s + 1) * LANES, n * WIDE : (n + 1) * WIDE] = jnp.where(
                kind, 1.0, 0.0
            ).astype(BF16)


def weigh(list_ref, blocks, stats, flat, table, picked, placing, stage, diagonal):
    for s in range(3):
        flat[s * MEM * OWN * 16 : (s + 1) * MEM * OWN * 16] = (
            blocks[s].astype(F32).reshape(MEM * OWN * 16, LANES)
        )
    blank = jnp.zeros((LANES - MEMBERS - 4, LANES), F32)

    def turn(k, carry):
        for s in range(3):
            cells = flat[pl.ds(s * MEM * OWN * 16 + k, MEMBERS, stride=16), :]
            extra = [stats[s, kind, pl.ds(k, 1), :] for kind in range(2)]
            high = [v.astype(BF16).astype(F32) for v in extra]
            low = [v - h for v, h in zip(extra, high)]
            whole = jnp.concatenate([cells] + high + low + [blank], axis=0)
            start = pl.multiple_of(s * OBS + k * LANES, LANES)
            table[pl.ds(start, LANES), :] = whole.T
        return carry

    lax.fori_loop(0, 16, turn, 0)

    def gather(q, carry):
        base = q * OBS_COL
        for s in range(GROUP):
            for o in range(OBS_COL):
                index = list_ref[q * GROUP + s, 0, o]
                picked[s, pl.ds(base + o, 1), :] = table[pl.ds(index, 1), :]
        return carry

    lax.fori_loop(0, GROUPS, gather, 0)
    found = jnp.concatenate([picked[s].astype(BF16) for s in range(GROUP)], axis=1)
    stage[...] = dot(found, placing[...])

    eye = jnp.zeros((MEMBERS, WIDE), F32)
    row48 = lax.broadcasted_iota(jnp.int32, (MEMBERS, WIDE), 0)
    col48 = lax.broadcasted_iota(jnp.int32, (MEMBERS, WIDE), 1)
    for s in range(GROUP):
        eye = jnp.where(col48 - MEMBERS * s == row48, 1.0, eye)
    lane = lax.broadcasted_iota(jnp.int32, (1, WIDE), 1)
    block48 = [(lane >= s * MEMBERS) & (lane < (s + 1) * MEMBERS) for s in range(GROUP)]
    every = range(GROUPS)

    def block_sum(pieces):
        return dot(jnp.concatenate(pieces, axis=0), diagonal[...])

    grams, proj, traces = [], [], []
    for q in every:
        rows = slice(q * OBS_COL, (q + 1) * OBS_COL)
        mean = stage[rows, WIDE : 2 * WIDE] * (1.0 / MEMBERS)
        pert = stage[rows, :WIDE] - mean
        depart = stage[rows, 2 * WIDE : 3 * WIDE] - mean
        scaled = pert * stage[rows, 3 * WIDE :]
        proj.append(jnp.sum(scaled * depart, axis=0, keepdims=True))
        traces.append(jnp.sum(scaled * pert, axis=0, keepdims=True))
        high, low = split(pert)
        scaled_high, scaled_low = split(scaled)
        square = lax.dot_general(
            jnp.concatenate([scaled_high, scaled_low, scaled_high], axis=0),
            jnp.concatenate([high, high, low], axis=0),
            (((0,), (0,)), ((), ())),
            preferred_element_type=F32,
        )
        gram = (MEMBERS - 1.0) * eye
        for s in range(GROUP):
            piece = square[s * MEMBERS : (s + 1) * MEMBERS]
            gram = gram + jnp.where(block48[s], piece, 0.0)
        grams.append(gram)
    trace = jnp.concatenate(traces + [jnp.zeros((16 - GROUPS, WIDE), F32)], axis=0)
    one = trace.astype(BF16)
    two, three = split(trace - one.astype(F32))
    sums = block_sum([one, two, three])
    scales = MEMBERS * (MEMBERS - 1.0) + sums[:16] + sums[16:32] + sums[32:]
    invert, reroot = 1.0 / scales, lax.rsqrt(scales)

    def times(parts, high, low):
        count = len(parts)
        first = dot(jnp.concatenate([x for pair in parts for x in pair], axis=0), high)
        second = dot(jnp.concatenate([pair[0] for pair in parts], axis=0), low)
        size = parts[0][0].shape[0]
        return [
            first[2 * n * size : (2 * n + 1) * size]
            + first[(2 * n + 1) * size : (2 * n + 2) * size]
            + second[n * size : (n + 1) * size]
            for n in range(count)
        ]

    def lay(pair):
        return [spread(piece) * diagonal[...] for piece in pair]

    ratio = [grams[q] * invert[q : q + 1] for q in every]
    inverse = [None] * GROUPS
    for sweep in range(SWEEPS):
        factor = [1.5 * eye - 0.5 * r for r in ratio]
        weights = [lay(split(f)) for f in factor]
        products = []
        for q in every:
            todo = []
            if sweep < SWEEPS - 1:
                todo.append(split(ratio[q]))
            if sweep > 0:
                todo.append(split(inverse[q]))
            products.append(times(todo, *weights[q]))
        inverse = [products[q][-1] if sweep > 0 else factor[q] for q in every]
        if sweep < SWEEPS - 1:
            ratio = [times([split(products[q][0])], *weights[q])[0] for q in every]

    root = [inverse[q] * reroot[q : q + 1] for q in every]
    weights = [lay(split(r)) for r in root]
    vector = proj
    spot = lax.broadcasted_iota(jnp.int32, (16, WIDE), 0)
    for _ in range(2):
        rows = []
        for q in every:
            high = vector[q].astype(BF16).astype(F32)
            low = vector[q] - high
            rows.append(jnp.where(spot == 0, high, jnp.where(spot == 1, low, 0.0)).astype(BF16))
        first = [dot(rows[q], weights[q][0]) for q in every]
        second = [dot(rows[q], weights[q][1]) for q in every]
        vector = [first[q][0:1] + first[q][1:2] + second[q][0:1] for q in every]
    transform = [(MEMBERS - 1.0) ** 0.5 * root[q] + vector[q] for q in every]
    sums = block_sum([piece for t in transform for piece in split(t)])
    pieces = []
    for q in every:
        at = 2 * q * MEMBERS
        both = sums[at : at + MEMBERS] + sums[at + MEMBERS : at + 2 * MEMBERS]
        pieces.append(lay(split(transform[q] + (1.0 - both) * (1.0 / MEMBERS))))
    return pieces


def apply(pieces, states, edges, unpack, columns, done, out):
    for source in range(MEM):
        for g in range(SETS):
            parts = dot(states[source, :, g * WIDE : (g + 1) * WIDE], unpack[...])
            for r in range(PACK):
                columns[pl.ds(source * OWN + g * PACK + r, SLOT, stride=MEMBERS), :] = parts[
                    :, r * LANES : (r + 1) * LANES
                ]
    ends = edges[...].astype(F32)
    for g in range(SETS):
        sides = [
            jnp.concatenate([ends[:, 4 * g + side, :], ends[:, 4 * g + 2 + side, :]], axis=1)
            for side in range(2)
        ]
        parts = dot(jnp.concatenate(sides, axis=0).astype(BF16), unpack[...])
        for side, column in ((0, 0), (1, WIDTH - 1)):
            for r in range(PACK):
                columns[pl.ds(column * MEMBERS + g * PACK + r, MEM, stride=OWN), :] = parts[
                    side * MEM : (side + 1) * MEM, r * LANES : (r + 1) * LANES
                ]

    for q in range(GROUPS):
        field = columns[q * GROUP * MEMBERS : q * GROUP * MEMBERS + WIDE, :].astype(BF16)
        result = dot(pieces[q][0], field) + dot(pieces[q][1], field)
        for s in range(GROUP):
            done[pl.ds(q * GROUP + s, MEMBERS, stride=WIDTH), :] = result[
                s * MEMBERS : (s + 1) * MEMBERS
            ]
    out[...] = done[:, :CHANS]


def exchange_kernel(
    lat_hbm, w_hbm, bias_hbm, cell_hbm, value_hbm, weight_hbm, list_hbm,
    out,
    lat_ref, w_ref, bias_ref, cell_ref, list_ref, blocks, stats, states, edges,
    field, act, wpad, taps, total, halves, turned, cellp, cellc,
    own, edge_out, edge_in, rows_out, ends, ends_out,
    flat, table, picked, placing, stage, columns, diagonal, unpack, done,
    loaded, edge_sent, edge_got, stat_sent, stat_got, mate_sent, sib_sent, outer_sent, block_got,
    state_sent, state_got, end_sent, end_got,
):
    m = lax.axis_index("mem")
    t = lax.axis_index("lon")
    tiles = lax.axis_size("lon")
    core = lax.rem(t, 2)
    left = lax.rem(t + tiles - 1, tiles)
    right = lax.rem(t + 1, tiles)
    outer = jnp.where(core == 0, left, right)
    inner = jnp.where(core == 0, right, left)
    mine, theirs = 2 * core, 2 - 2 * core
    far = lax.rem(jnp.where(core == 0, t, t + 1), tiles // 2) == 0

    barrier = pltpu.get_barrier_semaphore()
    for lon in (left, right):
        pl.semaphore_signal(barrier, inc=1, device_id={"lon": lon}, device_id_type=MESH)

    @pl.when(far)
    def _():
        for step in range(1, MEM):
            to = {"mem": lax.rem(m + step, MEM), "lon": outer}
            pl.semaphore_signal(barrier, inc=1, device_id=to, device_id_type=MESH)

    for step in range(1, MEM):
        to = {"mem": lax.rem(m + step, MEM)}
        pl.semaphore_signal(barrier, inc=1, device_id=to, device_id_type=MESH)

    loads = [
        pltpu.make_async_copy(source, target, loaded.at[n])
        for n, (source, target) in enumerate(
            (
                (lat_hbm, lat_ref),
                (w_hbm, w_ref),
                (bias_hbm, bias_ref),
                (cell_hbm, cell_ref),
                (value_hbm, stats.at[1, 0]),
                (weight_hbm, stats.at[1, 1]),
                (list_hbm, list_ref),
            )
        )
    ]
    for load in loads:
        load.start()

    edge_out[...] = jnp.zeros_like(edge_out)
    field[...] = jnp.zeros_like(field)
    wpad[...] = jnp.zeros_like(wpad)
    ends[...] = jnp.zeros_like(ends)
    build_constants(placing, diagonal, unpack)
    for load in loads[:-1]:
        load.wait()
    for side, column in ((0, WIDTH - 1), (1, 0)):
        edge = lat_ref[:, column].astype(F32).reshape(OWN * LAT, CHANS)
        edge_out[side, :, :CHANS] = edge.astype(BF16)

    lane = lax.broadcasted_iota(jnp.int32, (LANES, WIDE), 1)
    depth = lax.broadcasted_iota(jnp.int32, (LANES, WIDE), 0)
    blank = jnp.zeros((LANES, LANES), F32)
    for a in range(3):
        for b in range(3):
            wpad[:CHANS, :CHANS] = w_ref[a, b].astype(F32)
            whole = jnp.concatenate([wpad[...], blank], axis=1)
            for r in range(PACK):
                moved = whole if r == 0 else pltpu.roll(whole, CHANS * r, 1)
                taps[r, b * LANES : (b + 1) * LANES, a * WIDE : (a + 1) * WIDE] = moved.astype(BF16)
    for r in range(PACK):
        same = jnp.where((lane - CHANS * r == depth) & (depth < CHANS), 1.0, 0.0)
        taps[r, 3 * LANES :, :WIDE] = jnp.zeros((LANES, WIDE), BF16)
        taps[r, 3 * LANES :, WIDE : 2 * WIDE] = same.astype(BF16)
        taps[r, 3 * LANES :, 2 * WIDE :] = jnp.zeros((LANES, WIDE), BF16)
    wpad[:1, :CHANS] = bias_ref[...]
    bias = jnp.concatenate([wpad[:8, :], blank[:8, :]], axis=1)
    bias = bias + pltpu.roll(bias, CHANS, 1) + pltpu.roll(bias, 2 * CHANS, 1)
    bias = jnp.where(lane[:8, :] < PACK * CHANS, bias, 0.0)[:1, :]

    named = cell_ref[...]
    pixel = jnp.floor((named.astype(F32) + 0.5) * (1.0 / CHANS)).astype(jnp.int32)
    row = jnp.floor((pixel.astype(F32) + 0.5) * (1.0 / WIDTH)).astype(jnp.int32)
    cellc[...] = named - CHANS * pixel
    cellp[...] = (pixel - WIDTH * row) * LAT + row

    pl.semaphore_wait(barrier, jnp.where(far, 2 * MEM, MEM + 1))

    edge_copies = [
        pltpu.make_async_remote_copy(
            src_ref=edge_out.at[side],
            dst_ref=edge_in.at[side],
            send_sem=edge_sent.at[side],
            recv_sem=edge_got.at[side],
            device_id={"lon": lon},
            device_id_type=MESH,
        )
        for side, lon in ((0, right), (1, left))
    ]
    stat_copies = [
        pltpu.make_async_remote_copy(
            src_ref=stats.at[1],
            dst_ref=stats.at[2 * side],
            send_sem=stat_sent.at[side],
            recv_sem=stat_got.at[side],
            device_id={"lon": lon},
            device_id_type=MESH,
        )
        for side, lon in ((0, right), (1, left))
    ]
    for copy in edge_copies + stat_copies:
        copy.start()

    for k in range(OWN):
        field[k, LAT : LAT + CELLS, :CHANS] = lat_ref[k].astype(F32).reshape(CELLS, CHANS)
    act[...] = silu(field[...])

    span = CELLS + LAT
    for g in range(SETS):
        parts = None
        for r in range(PACK):
            k = PACK * g + r
            sides = [act[k, LAT * b : LAT * b + span, :].astype(BF16) for b in range(3)]
            sides.append(field[k, LAT : LAT + span, :].astype(BF16))
            part = dot(jnp.concatenate(sides, axis=1), taps[r])
            parts = part if parts is None else parts + part
        summed = combine(parts) + bias
        total[g, :span] = summed
        total[g, span:] = jnp.zeros((BAND - span, WIDE), F32)
        for h in range(2):
            halves[2 * g + h] = total[g, :, h * LANES : (h + 1) * LANES]

    for i in range(LAT):
        for half in range(2 * SETS):
            rows_out[i, :, half * LANES : (half + 1) * LANES] = halves[
                half, pl.ds(i, SLOT, stride=LAT), :
            ].astype(BF16)
    states[m] = rows_out[m]

    def row_copy(to, source):
        return pltpu.make_async_remote_copy(
            src_ref=rows_out.at[to],
            dst_ref=states.at[source],
            send_sem=state_sent.at[to],
            recv_sem=state_got.at[source],
            device_id={"mem": to},
            device_id_type=MESH,
        )

    def end_copy(to, source):
        return pltpu.make_async_remote_copy(
            src_ref=ends_out.at[to],
            dst_ref=edges.at[source],
            send_sem=end_sent.at[to],
            recv_sem=end_got.at[source],
            device_id={"mem": to},
            device_id_type=MESH,
        )


    for side, copy in enumerate(edge_copies):
        copy.wait_recv()
        turn = silu(edge_in[side].astype(F32)).astype(BF16).astype(F32)
        parts = None
        for r in range(PACK):
            pick = [turn[(PACK * g + r) * LAT : (PACK * g + r + 1) * LAT] for g in range(SETS)]
            tap = 2 * side
            part = dot(
                jnp.concatenate(pick, axis=0).astype(BF16), taps[r, tap * LANES : (tap + 1) * LANES]
            )
            parts = part if parts is None else parts + part
        extra = combine(parts)
        first = 0 if side == 0 else CELLS - LAT
        for g in range(SETS):
            total[g, first : first + LAT] += extra[g * LAT : (g + 1) * LAT]
            for h in range(2):
                ends[pl.ds(4 * g + 2 * h + side, LAT, stride=16), :] = total[
                    g, first : first + LAT, h * LANES : (h + 1) * LANES
                ]
    ends_out[...] = ends[...].astype(BF16).reshape(LAT, 16, LANES)
    edges[m] = ends_out[m]
    for g in range(SETS):
        turned[g * WIDE : (g + 1) * WIDE] = total[g].T.astype(BF16)

    place = lax.broadcasted_iota(jnp.int32, (BAND, LANES), 0)
    channel = lax.broadcasted_iota(jnp.int32, (WIDE, WIDE), 0)

    def choose(pair, carry):
        first = cellp[pl.ds(2 * pair, 1), :]
        second = cellp[pl.ds(2 * pair + 1, 1), :]
        hot = jnp.concatenate(
            [
                jnp.where(place == first, 1.0, 0.0).astype(BF16),
                jnp.where(place == second, 1.0, 0.0).astype(BF16),
            ],
            axis=1,
        )
        chans = jnp.concatenate(
            [cellc[pl.ds(2 * pair, 1), :], cellc[pl.ds(2 * pair + 1, 1), :]], axis=1
        )
        for g in range(SETS):
            cells = dot(turned[g * WIDE : (g + 1) * WIDE, :], hot)
            for r in range(PACK):
                low, high = CHANS * r // 8 * 8, -(-CHANS * (r + 1) // 8) * 8
                mask = channel[low:high] - CHANS * r == chans
                found = jnp.sum(jnp.where(mask, cells[low:high], 0.0), axis=0, keepdims=True)
                spot = (PACK * g + r) * 16 + 2 * pair
                own[pl.ds(spot, 1), :] = found[:, :LANES]
                own[pl.ds(spot + 1, 1), :] = found[:, LANES:]
        return carry

    lax.fori_loop(0, OBS // WIDE, choose, 0)
    blocks[1, m] = own[...].astype(BF16)

    def arrival(slot, block):
        return pltpu.make_async_remote_copy(
            src_ref=blocks.at[1, block],
            dst_ref=blocks.at[slot, block],
            send_sem=sib_sent.at[block],
            recv_sem=block_got.at[slot, block],
            device_id={"lon": inner},
            device_id_type=MESH,
        )

    def along(block, sent, to):
        return pltpu.make_async_remote_copy(
            src_ref=blocks.at[1, block],
            dst_ref=blocks.at[1, block],
            send_sem=mate_sent.at[sent],
            recv_sem=block_got.at[1, block],
            device_id={"mem": to},
            device_id_type=MESH,
        )

    def across(block):
        return pltpu.make_async_remote_copy(
            src_ref=blocks.at[1, block],
            dst_ref=blocks.at[mine, block],
            send_sem=sib_sent.at[block],
            recv_sem=block_got.at[mine, block],
            device_id={"lon": inner},
            device_id_type=MESH,
        )

    def outward(block, sent, to):
        return pltpu.make_async_remote_copy(
            src_ref=blocks.at[1, block],
            dst_ref=blocks.at[theirs, block],
            send_sem=outer_sent.at[sent],
            recv_sem=block_got.at[theirs, block],
            device_id={"mem": to, "lon": outer},
            device_id_type=MESH,
        )

    half = m // 4 * 4
    partner = lax.rem(m + 4, MEM)
    partner_half = 4 - half
    mates = [half + lax.rem(m + step, 4) for step in range(1, 4)]
    partner_mates = [partner_half + lax.rem(m + step, 4) for step in range(1, 4)]

    @pl.when(far)
    def _():
        for step in range(MEM):
            to = lax.rem(m + step, MEM)
            outward(m, to, to).start()

    def pass_on(block):
        across(block).start()

        @pl.when(jnp.logical_not(far))
        def _():
            outward(block, block, m).start()

    along(m, 3, partner).start()
    for n in range(3):
        along(m, n, mates[n]).start()
    pass_on(m)
    for step in range(1, MEM):
        end_copy(lax.rem(m + step, MEM), m).start()
    for n in range(3):
        arrival(1, mates[n]).wait_recv()
        pass_on(mates[n])
    arrival(1, partner).wait_recv()
    for n in range(3):
        along(partner, 4 + n, mates[n]).start()
    pass_on(partner)
    for n in range(3):
        arrival(1, partner_mates[n]).wait_recv()
        pass_on(partner_mates[n])

    for step in range(1, MEM):
        row_copy(lax.rem(m + step, MEM), m).start()
    for block in range(MEM):
        arrival(mine, block).wait_recv()
        arrival(theirs, block).wait_recv()
    for copy in stat_copies:
        copy.wait()
    loads[-1].wait()
    pieces = weigh(list_ref, blocks, stats, flat, table, picked, placing, stage, diagonal)

    for step in range(1, MEM):
        other = lax.rem(m + step, MEM)
        row_copy(other, other).wait_recv()
        end_copy(other, other).wait_recv()
    apply(pieces, states, edges, unpack, columns, done, out)

    for copy in edge_copies:
        copy.wait_send()
    for block in range(MEM):
        across(block).wait_send()
        outward(block, block, m).wait_send()
    along(m, 3, partner).wait_send()
    for n in range(3):
        along(m, n, mates[n]).wait_send()
        along(partner, 4 + n, mates[n]).wait_send()
    for step in range(1, MEM):
        other = lax.rem(m + step, MEM)
        row_copy(other, other).wait_send()
        end_copy(other, other).wait_send()


def exchange(lat, weights, bias, cell, value, weight, lists):
    hbm = pl.BlockSpec(memory_space=pltpu.HBM)
    vmem = pl.BlockSpec(memory_space=pltpu.VMEM)
    dma = pltpu.SemaphoreType.DMA
    return pl.pallas_call(
        exchange_kernel,
        out_shape=jax.ShapeDtypeStruct((MEMBERS * WIDTH, CHANS), F32),
        in_specs=[hbm] * 7,
        out_specs=vmem,
        scratch_shapes=[
            pltpu.VMEM(lat.shape, BF16),
            pltpu.VMEM(weights.shape, BF16),
            pltpu.VMEM(bias.shape, F32),
            pltpu.VMEM(cell.shape, jnp.int32),
            pltpu.SMEM(lists.shape, jnp.int32),
            pltpu.VMEM((3, MEM, OWN * 16, LANES), BF16),
            pltpu.VMEM((3, 2, 16, LANES), F32),
            pltpu.VMEM((MEM, SLOT, SETS * WIDE), BF16),
            pltpu.VMEM((MEM, 16, LANES), BF16),
            pltpu.VMEM((OWN, BAND, LANES), F32),
            pltpu.VMEM((OWN, BAND, LANES), F32),
            pltpu.VMEM((LANES, LANES), F32),
            pltpu.VMEM((PACK, 4 * LANES, 3 * WIDE), BF16),
            pltpu.VMEM((SETS, BAND, WIDE), F32),
            pltpu.VMEM((2 * SETS, BAND, LANES), F32),
            pltpu.VMEM((SETS * WIDE, BAND), BF16),
            pltpu.VMEM((16, LANES), jnp.int32),
            pltpu.VMEM((16, LANES), jnp.int32),
            pltpu.VMEM((OWN * 16, LANES), F32),
            pltpu.VMEM((2, OWN * LAT, LANES), BF16),
            pltpu.VMEM((2, OWN * LAT, LANES), BF16),
            pltpu.VMEM((LAT, SLOT, SETS * WIDE), BF16),
            pltpu.VMEM((LAT * 16, LANES), F32),
            pltpu.VMEM((LAT, 16, LANES), BF16),
            pltpu.VMEM((3 * MEM * OWN * 16, LANES), F32),
            pltpu.VMEM((3 * OBS, LANES), F32),
            pltpu.VMEM((GROUP, GROUPS * OBS_COL, LANES), F32),
            pltpu.VMEM((GROUP * LANES, 4 * WIDE), BF16),
            pltpu.VMEM((GROUPS * OBS_COL, 4 * WIDE), F32),
            pltpu.VMEM((SLOT * MEMBERS, LANES), F32),
            pltpu.VMEM((WIDE, WIDE), BF16),
            pltpu.VMEM((WIDE, PACK * LANES), BF16),
            pltpu.VMEM((MEMBERS * WIDTH, LANES), F32),
            dma((7,)),
            dma((2,)),
            dma((2,)),
            dma((2,)),
            dma((2,)),
            dma((7,)),
            dma((MEM,)),
            dma((MEM,)),
            dma((3, MEM)),
            dma((MEM,)),
            dma((MEM,)),
            dma((MEM,)),
            dma((MEM,)),
        ],
        compiler_params=pltpu.CompilerParams(
            collective_id=0, has_side_effects=True, vmem_limit_bytes=60 * 2**20
        ),
    )(lat, weights, bias, cell, value, weight, lists)


def local(latent, conv_weight, conv_bias, obs_cell, obs_value, obs_weight, obs_list):
    result = exchange(
        jnp.transpose(latent, (0, 2, 1, 3)),
        conv_weight,
        conv_bias.reshape(1, CHANS),
        obs_cell.reshape(16, LANES),
        obs_value.reshape(16, LANES),
        obs_weight.reshape(16, LANES),
        obs_list.reshape(WIDTH, 1, OBS_COL),
    )
    return jnp.transpose(result.reshape(MEMBERS, WIDTH, 1, CHANS), (0, 2, 1, 3))


def solution(mesh):
    placed = (
        P("mem", None, "lon", None),
        P(),
        P(),
        P("lon"),
        P("lon"),
        P("lon"),
        P("mem", "lon", None),
    )
    return jax.shard_map(
        local, mesh=mesh, in_specs=placed, out_specs=P(None, "mem", "lon", None), check_vma=False
    )
```

```python
import functools

import jax
import jax.numpy as jnp
from jax import lax
from jax.experimental import pallas as pl
from jax.experimental.pallas import tpu as pltpu
from jax.sharding import PartitionSpec as P

SWEEPS = 6
MEM = 8
MEMBERS = 48
CHANS = 78
WIDTH = 45
LAT = 8
OWN = 6
PACK = 3
SETS = OWN // PACK
OBS = 2048
OBS_COL = 64
LANES = 128
GROUP = 5
GROUPS = WIDTH // GROUP
CELLS = WIDTH * LAT
BAND = 384
WIDE = 2 * LANES
SLOT = 48
EARLY = (3, 4, 5)
LATE = (1, 2, 6, 7)
F32 = jnp.float32
BF16 = jnp.bfloat16
MESH = pl.DeviceIdType.MESH


def dot(left, right):
    return jnp.dot(left, right, preferred_element_type=F32)


def silu(v):
    return v / (1.0 + jnp.exp(-v))


def split(v):
    high = v.astype(BF16)
    return high, (v - high.astype(F32)).astype(BF16)


def combine(parts):
    rows = parts.shape[0]
    cube = parts.reshape(rows // LAT, LAT, 3 * WIDE)
    spot = lax.broadcasted_iota(jnp.int32, (rows // LAT, LAT, WIDE), 1)
    above = pltpu.roll(cube[:, :, :WIDE], 1, 1)
    below = pltpu.roll(cube[:, :, 2 * WIDE :], LAT - 1, 1)
    total = cube[:, :, WIDE : 2 * WIDE]
    total = total + jnp.where(spot > 0, above, 0.0) + jnp.where(spot < LAT - 1, below, 0.0)
    return total.reshape(rows, WIDE)


def spread(piece):
    return jnp.concatenate([piece] * GROUP + [jnp.zeros((16, WIDE), BF16)], axis=0)


def build_constants(placing, diagonal, unpack):
    row = lax.broadcasted_iota(jnp.int32, (WIDE, WIDE), 0)
    col = lax.broadcasted_iota(jnp.int32, (WIDE, WIDE), 1)
    mask = jnp.zeros((WIDE, WIDE), F32)
    for s in range(GROUP):
        low, high = s * MEMBERS, (s + 1) * MEMBERS
        mask = jnp.where((row >= low) & (row < high) & (col >= low) & (col < high), 1.0, mask)
    diagonal[...] = mask.astype(BF16)
    row = lax.broadcasted_iota(jnp.int32, (WIDE, LANES), 0)
    col = lax.broadcasted_iota(jnp.int32, (WIDE, LANES), 1)
    for r in range(PACK):
        unpack[:, r * LANES : (r + 1) * LANES] = jnp.where(
            (row - CHANS * r == col) & (col < CHANS), 1.0, 0.0
        ).astype(BF16)
    row = lax.broadcasted_iota(jnp.int32, (LANES, WIDE), 0)
    col = lax.broadcasted_iota(jnp.int32, (LANES, WIDE), 1)
    member = row < MEMBERS
    for s in range(GROUP):
        inside = (col >= s * MEMBERS) & (col < (s + 1) * MEMBERS)
        kinds = (
            member & (col - s * MEMBERS == row),
            member & inside,
            ((row == MEMBERS) | (row == MEMBERS + 2)) & inside,
            ((row == MEMBERS + 1) | (row == MEMBERS + 3)) & inside,
        )
        for n, kind in enumerate(kinds):
            placing[s * LANES : (s + 1) * LANES, n * WIDE : (n + 1) * WIDE] = jnp.where(
                kind, 1.0, 0.0
            ).astype(BF16)


def fill(slot, blocks, stats, flat, table):
    flat[...] = blocks[slot].astype(F32).reshape(MEM * OWN * 16, LANES)
    blank = jnp.zeros((LANES - MEMBERS - 4, LANES), F32)

    def turn(k, carry):
        cells = flat[pl.ds(k, MEMBERS, stride=16), :]
        extra = [stats[slot, kind, pl.ds(k, 1), :] for kind in range(2)]
        high = [v.astype(BF16).astype(F32) for v in extra]
        low = [v - h for v, h in zip(extra, high)]
        whole = jnp.concatenate([cells] + high + low + [blank], axis=0)
        start = pl.multiple_of(slot * OBS + k * LANES, LANES)
        table[pl.ds(start, LANES), :] = whole.T
        return carry

    lax.fori_loop(0, 16, turn, 0, unroll=8)


def weigh(list_ref, table, picked, placing, stage, diagonal):
    def gather(q, carry):
        base = q * OBS_COL
        for s in range(GROUP):
            for o in range(OBS_COL):
                index = list_ref[q * GROUP + s, 0, o]
                picked[s, pl.ds(base + o, 1), :] = table[pl.ds(index, 1), :]
        return carry

    lax.fori_loop(0, GROUPS, gather, 0)
    found = jnp.concatenate([picked[s].astype(BF16) for s in range(GROUP)], axis=1)
    stage[...] = dot(found, placing[...])

    eye = jnp.zeros((MEMBERS, WIDE), F32)
    row48 = lax.broadcasted_iota(jnp.int32, (MEMBERS, WIDE), 0)
    col48 = lax.broadcasted_iota(jnp.int32, (MEMBERS, WIDE), 1)
    for s in range(GROUP):
        eye = jnp.where(col48 - MEMBERS * s == row48, 1.0, eye)
    lane = lax.broadcasted_iota(jnp.int32, (1, WIDE), 1)
    block48 = [(lane >= s * MEMBERS) & (lane < (s + 1) * MEMBERS) for s in range(GROUP)]
    every = range(GROUPS)

    def block_sum(pieces):
        return dot(jnp.concatenate(pieces, axis=0), diagonal[...])

    grams, proj, traces = [], [], []
    for q in every:
        rows = slice(q * OBS_COL, (q + 1) * OBS_COL)
        mean = stage[rows, WIDE : 2 * WIDE] * (1.0 / MEMBERS)
        pert = stage[rows, :WIDE] - mean
        depart = stage[rows, 2 * WIDE : 3 * WIDE] - mean
        scaled = pert * stage[rows, 3 * WIDE :]
        proj.append(jnp.sum(scaled * depart, axis=0, keepdims=True))
        traces.append(jnp.sum(scaled * pert, axis=0, keepdims=True))
        high, low = split(pert)
        scaled_high, scaled_low = split(scaled)
        square = lax.dot_general(
            jnp.concatenate([scaled_high, scaled_low, scaled_high], axis=0),
            jnp.concatenate([high, high, low], axis=0),
            (((0,), (0,)), ((), ())),
            preferred_element_type=F32,
        )
        gram = (MEMBERS - 1.0) * eye
        for s in range(GROUP):
            piece = square[s * MEMBERS : (s + 1) * MEMBERS]
            gram = gram + jnp.where(block48[s], piece, 0.0)
        grams.append(gram)
    trace = jnp.concatenate(traces + [jnp.zeros((16 - GROUPS, WIDE), F32)], axis=0)
    one = trace.astype(BF16)
    two, three = split(trace - one.astype(F32))
    sums = block_sum([one, two, three])
    scales = MEMBERS * (MEMBERS - 1.0) + sums[:16] + sums[16:32] + sums[32:]
    invert, reroot = 1.0 / scales, lax.rsqrt(scales)

    def times(parts, high, low):
        count = len(parts)
        first = dot(jnp.concatenate([x for pair in parts for x in pair], axis=0), high)
        second = dot(jnp.concatenate([pair[0] for pair in parts], axis=0), low)
        size = parts[0][0].shape[0]
        return [
            first[2 * n * size : (2 * n + 1) * size]
            + first[(2 * n + 1) * size : (2 * n + 2) * size]
            + second[n * size : (n + 1) * size]
            for n in range(count)
        ]

    def lay(pair):
        return [spread(piece) * diagonal[...] for piece in pair]

    ratio = [grams[q] * invert[q : q + 1] for q in every]
    inverse = [None] * GROUPS
    for sweep in range(SWEEPS):
        factor = [1.5 * eye - 0.5 * r for r in ratio]
        weights = [lay(split(f)) for f in factor]
        products = []
        for q in every:
            todo = []
            if sweep < SWEEPS - 1:
                todo.append(split(ratio[q]))
            if sweep > 0:
                todo.append(split(inverse[q]))
            products.append(times(todo, *weights[q]))
        inverse = [products[q][-1] if sweep > 0 else factor[q] for q in every]
        if sweep < SWEEPS - 1:
            ratio = [times([split(products[q][0])], *weights[q])[0] for q in every]

    root = [inverse[q] * reroot[q : q + 1] for q in every]
    weights = [lay(split(r)) for r in root]
    vector = proj
    spot = lax.broadcasted_iota(jnp.int32, (16, WIDE), 0)
    for _ in range(2):
        rows = []
        for q in every:
            high = vector[q].astype(BF16).astype(F32)
            low = vector[q] - high
            rows.append(jnp.where(spot == 0, high, jnp.where(spot == 1, low, 0.0)).astype(BF16))
        first = [dot(rows[q], weights[q][0]) for q in every]
        second = [dot(rows[q], weights[q][1]) for q in every]
        vector = [first[q][0:1] + first[q][1:2] + second[q][0:1] for q in every]
    transform = [(MEMBERS - 1.0) ** 0.5 * root[q] + vector[q] for q in every]
    sums = block_sum([piece for t in transform for piece in split(t)])
    pieces = []
    for q in every:
        at = 2 * q * MEMBERS
        both = sums[at : at + MEMBERS] + sums[at + MEMBERS : at + 2 * MEMBERS]
        pieces.append(lay(split(transform[q] + (1.0 - both) * (1.0 / MEMBERS))))
    return pieces


def apply(pieces, states, edges, unpack, columns, done, out):
    for source in range(MEM):
        for g in range(SETS):
            parts = dot(states[source, :, g * WIDE : (g + 1) * WIDE], unpack[...])
            for r in range(PACK):
                columns[pl.ds(source * OWN + g * PACK + r, SLOT, stride=MEMBERS), :] = parts[
                    :, r * LANES : (r + 1) * LANES
                ]
    ends = edges[...].astype(F32)
    for g in range(SETS):
        sides = [
            jnp.concatenate([ends[:, 4 * g + side, :], ends[:, 4 * g + 2 + side, :]], axis=1)
            for side in range(2)
        ]
        parts = dot(jnp.concatenate(sides, axis=0).astype(BF16), unpack[...])
        for side, column in ((0, 0), (1, WIDTH - 1)):
            for r in range(PACK):
                columns[pl.ds(column * MEMBERS + g * PACK + r, MEM, stride=OWN), :] = parts[
                    side * MEM : (side + 1) * MEM, r * LANES : (r + 1) * LANES
                ]

    for q in range(GROUPS):
        field = columns[q * GROUP * MEMBERS : q * GROUP * MEMBERS + WIDE, :].astype(BF16)
        result = dot(pieces[q][0], field) + dot(pieces[q][1], field)
        for s in range(GROUP):
            done[pl.ds(q * GROUP + s, MEMBERS, stride=WIDTH), :] = result[
                s * MEMBERS : (s + 1) * MEMBERS
            ]
    out[...] = done[:, :CHANS]


def exchange_kernel(
    lat_hbm, w_hbm, bias_hbm, cell_hbm, value_hbm, weight_hbm, list_hbm,
    out,
    lat_ref, w_ref, bias_ref, cell_ref, list_ref, blocks, stats, states, edges,
    field, act, wpad, taps, total, halves, turned, turned_rim, cellp, cellc,
    own, edge_out, edge_in, rows_out, ends, ends_out,
    flat, table, picked, placing, stage, columns, diagonal, unpack, done,
    loaded, edge_sent, edge_got, stat_sent, stat_got, mate_sent, sib_sent, outer_sent, block_got,
    state_sent, state_got, end_sent, end_got,
):
    m = lax.axis_index("mem")
    t = lax.axis_index("lon")
    tiles = lax.axis_size("lon")
    core = lax.rem(t, 2)
    left = lax.rem(t + tiles - 1, tiles)
    right = lax.rem(t + 1, tiles)
    outer = jnp.where(core == 0, left, right)
    inner = jnp.where(core == 0, right, left)
    mine, theirs = 2 * core, 2 - 2 * core
    far = lax.rem(jnp.where(core == 0, t, t + 1), tiles // 2) == 0

    quarter, pair = tiles // 4, lax.rem(t // 2, tiles // 4)
    busy = (pair == 0) | (pair == quarter - 1)

    barrier = pltpu.get_barrier_semaphore()
    for lon in (left, right):
        pl.semaphore_signal(barrier, inc=1, device_id={"lon": lon}, device_id_type=MESH)

    @pl.when(far)
    def _():
        for step in range(1, MEM):
            to = {"mem": lax.rem(m + step, MEM), "lon": outer}
            pl.semaphore_signal(barrier, inc=1, device_id=to, device_id_type=MESH)

    for step in range(1, MEM):
        to = {"mem": lax.rem(m + step, MEM)}
        pl.semaphore_signal(barrier, inc=1, device_id=to, device_id_type=MESH)

    loads = [
        pltpu.make_async_copy(source, target, loaded.at[n])
        for n, (source, target) in enumerate(
            (
                (lat_hbm, lat_ref),
                (w_hbm, w_ref),
                (bias_hbm, bias_ref),
                (cell_hbm, cell_ref),
                (value_hbm, stats.at[1, 0]),
                (weight_hbm, stats.at[1, 1]),
                (list_hbm, list_ref),
            )
        )
    ]
    for load in loads:
        load.start()

    edge_out[...] = jnp.zeros_like(edge_out)
    field[...] = jnp.zeros_like(field)
    wpad[...] = jnp.zeros_like(wpad)
    ends[...] = jnp.zeros_like(ends)
    loads[0].wait()
    for side, column in ((0, WIDTH - 1), (1, 0)):
        edge = lat_ref[:, column].astype(F32).reshape(OWN * LAT, CHANS)
        edge_out[side, :, :CHANS] = edge.astype(BF16)

    for k in range(OWN):
        field[k, LAT : LAT + CELLS, :CHANS] = lat_ref[k].astype(F32).reshape(CELLS, CHANS)
    act[...] = silu(field[...])

    for load in loads[1:-1]:
        load.wait()
    lane = lax.broadcasted_iota(jnp.int32, (LANES, WIDE), 1)
    depth = lax.broadcasted_iota(jnp.int32, (LANES, WIDE), 0)
    blank = jnp.zeros((LANES, LANES), F32)
    for a in range(3):
        for b in range(3):
            wpad[:CHANS, :CHANS] = w_ref[a, b].astype(F32)
            whole = jnp.concatenate([wpad[...], blank], axis=1)
            for r in range(PACK):
                moved = whole if r == 0 else pltpu.roll(whole, CHANS * r, 1)
                taps[r, b * LANES : (b + 1) * LANES, a * WIDE : (a + 1) * WIDE] = moved.astype(BF16)
    for r in range(PACK):
        same = jnp.where((lane - CHANS * r == depth) & (depth < CHANS), 1.0, 0.0)
        taps[r, 3 * LANES :, :WIDE] = jnp.zeros((LANES, WIDE), BF16)
        taps[r, 3 * LANES :, WIDE : 2 * WIDE] = same.astype(BF16)
        taps[r, 3 * LANES :, 2 * WIDE :] = jnp.zeros((LANES, WIDE), BF16)
    wpad[:1, :CHANS] = bias_ref[...]
    bias = jnp.concatenate([wpad[:8, :], blank[:8, :]], axis=1)
    bias = bias + pltpu.roll(bias, CHANS, 1) + pltpu.roll(bias, 2 * CHANS, 1)
    bias = jnp.where(lane[:8, :] < PACK * CHANS, bias, 0.0)[:1, :]

    span = CELLS + LAT
    for g in range(SETS):
        parts = None
        for r in range(PACK):
            k = PACK * g + r
            sides = [act[k, LAT * b : LAT * b + span, :].astype(BF16) for b in range(3)]
            sides.append(field[k, LAT : LAT + span, :].astype(BF16))
            part = dot(jnp.concatenate(sides, axis=1), taps[r])
            parts = part if parts is None else parts + part
        summed = combine(parts) + bias
        total[g, :span] = summed
        total[g, span:] = jnp.zeros((BAND - span, WIDE), F32)
        for h in range(2):
            halves[2 * g + h] = total[g, :, h * LANES : (h + 1) * LANES]

    named = cell_ref[...]
    pixel = jnp.floor((named.astype(F32) + 0.5) * (1.0 / CHANS)).astype(jnp.int32)
    row = jnp.floor((pixel.astype(F32) + 0.5) * (1.0 / WIDTH)).astype(jnp.int32)
    cellc[...] = named - CHANS * pixel
    cellp[...] = (pixel - WIDTH * row) * LAT + row

    pl.semaphore_wait(barrier, jnp.where(far, 2 * MEM, MEM + 1))

    edge_copies = [
        pltpu.make_async_remote_copy(
            src_ref=edge_out.at[side],
            dst_ref=edge_in.at[side],
            send_sem=edge_sent.at[side],
            recv_sem=edge_got.at[side],
            device_id={"lon": lon},
            device_id_type=MESH,
        )
        for side, lon in ((0, right), (1, left))
    ]
    stat_copies = [
        pltpu.make_async_remote_copy(
            src_ref=stats.at[1],
            dst_ref=stats.at[2 * side],
            send_sem=stat_sent.at[side],
            recv_sem=stat_got.at[side],
            device_id={"lon": lon},
            device_id_type=MESH,
        )
        for side, lon in ((0, right), (1, left))
    ]
    for copy in edge_copies:
        copy.start()


    def mend(side):
        pltpu.make_async_remote_copy(
            src_ref=edge_out.at[side],
            dst_ref=edge_in.at[side],
            send_sem=edge_sent.at[side],
            recv_sem=edge_got.at[side],
            device_id={"lon": inner},
            device_id_type=MESH,
        ).wait_recv()
        turn = silu(edge_in[side].astype(F32)).astype(BF16).astype(F32)
        tap = pl.multiple_of(2 * side * LANES, LANES)
        parts = None
        for r in range(PACK):
            pick = [turn[(PACK * g + r) * LAT : (PACK * g + r + 1) * LAT] for g in range(SETS)]
            part = dot(jnp.concatenate(pick, axis=0).astype(BF16), taps[r, pl.ds(tap, LANES)])
            parts = part if parts is None else parts + part
        extra = combine(parts)
        first = pl.multiple_of(side * (CELLS - LAT), LAT)
        for g in range(SETS):
            edge = total[g, pl.ds(first, LAT)] + extra[g * LAT : (g + 1) * LAT]
            total[g, pl.ds(first, LAT)] = edge
            for h in range(2):
                ends[pl.ds(4 * g + 2 * h + side, LAT, stride=16), :] = edge[
                    :, h * LANES : (h + 1) * LANES
                ]

    for i in range(LAT):
        for half in range(2 * SETS):
            rows_out[i, :, half * LANES : (half + 1) * LANES] = halves[
                half, pl.ds(i, SLOT, stride=LAT), :
            ].astype(BF16)
    states[m] = rows_out[m]

    def row_copy(to, source):
        return pltpu.make_async_remote_copy(
            src_ref=rows_out.at[to],
            dst_ref=states.at[source],
            send_sem=state_sent.at[to],
            recv_sem=state_got.at[source],
            device_id={"mem": to},
            device_id_type=MESH,
        )

    def end_copy(to, source):
        return pltpu.make_async_remote_copy(
            src_ref=ends_out.at[to],
            dst_ref=edges.at[source],
            send_sem=end_sent.at[to],
            recv_sem=end_got.at[source],
            device_id={"mem": to},
            device_id_type=MESH,
        )


    @pl.when(busy)
    def _():
        for step in EARLY:
            row_copy(lax.rem(m + step, MEM), m).start()

    build_constants(placing, diagonal, unpack)
    channel = lax.broadcasted_iota(jnp.int32, (WIDE, WIDE), 0)
    rim = pl.multiple_of(jnp.where(core == 0, 0, CELLS - LAT), LAT)

    def choose_from(source, first_cell, more):
        place = lax.broadcasted_iota(jnp.int32, (source.shape[1], LANES), 0) + first_cell

        def choose(pair, carry):
            rows = [pl.ds(2 * pair + n, 1) for n in range(2)]
            hot = jnp.concatenate(
                [jnp.where(place == cellp[at, :], 1.0, 0.0).astype(BF16) for at in rows], axis=1
            )
            chans = jnp.concatenate([cellc[at, :] for at in rows], axis=1)
            for g in range(SETS):
                cells = dot(source[g * WIDE : (g + 1) * WIDE, :], hot)
                for r in range(PACK):
                    low, high = CHANS * r // 8 * 8, -(-CHANS * (r + 1) // 8) * 8
                    mask = channel[low:high] - CHANS * r == chans
                    found = jnp.sum(jnp.where(mask, cells[low:high], 0.0), axis=0, keepdims=True)
                    for n in range(2):
                        spot = pl.ds((PACK * g + r) * 16 + 2 * pair + n, 1)
                        piece = found[:, n * LANES : (n + 1) * LANES]
                        own[spot, :] = own[spot, :] + piece if more else piece
            return carry

        lax.fori_loop(0, OBS // WIDE, choose, 0, unroll=2)

    mend(1 - core)
    cell_row = lax.broadcasted_iota(jnp.int32, (BAND, WIDE), 0)
    for g in range(SETS):
        keep = (cell_row < rim) | (cell_row >= rim + LAT)
        turned[g * WIDE : (g + 1) * WIDE] = jnp.where(keep, total[g], 0.0).T.astype(BF16)
    choose_from(turned, 0, False)

    mend(core)
    for copy in stat_copies:
        copy.start()
    ends_out[...] = ends[...].astype(BF16).reshape(LAT, 16, LANES)
    edges[m] = ends_out[m]
    for g in range(SETS):
        edge = jnp.concatenate(
            [total[g, pl.ds(rim, LAT), :], jnp.zeros((LANES - LAT, WIDE), F32)], axis=0
        )
        turned_rim[g * WIDE : (g + 1) * WIDE] = edge.T.astype(BF16)
    choose_from(turned_rim, rim, True)
    blocks[1, m] = own[...].astype(BF16)

    def arrival(slot, block):
        return pltpu.make_async_remote_copy(
            src_ref=blocks.at[1, block],
            dst_ref=blocks.at[slot, block],
            send_sem=sib_sent.at[block],
            recv_sem=block_got.at[slot, block],
            device_id={"lon": inner},
            device_id_type=MESH,
        )

    def along(block, sent, to):
        return pltpu.make_async_remote_copy(
            src_ref=blocks.at[1, block],
            dst_ref=blocks.at[1, block],
            send_sem=mate_sent.at[sent],
            recv_sem=block_got.at[1, block],
            device_id={"mem": to},
            device_id_type=MESH,
        )

    def across(block):
        return pltpu.make_async_remote_copy(
            src_ref=blocks.at[1, block],
            dst_ref=blocks.at[mine, block],
            send_sem=sib_sent.at[block],
            recv_sem=block_got.at[mine, block],
            device_id={"lon": inner},
            device_id_type=MESH,
        )

    def outward(block, sent, to):
        return pltpu.make_async_remote_copy(
            src_ref=blocks.at[1, block],
            dst_ref=blocks.at[theirs, block],
            send_sem=outer_sent.at[sent],
            recv_sem=block_got.at[theirs, block],
            device_id={"mem": to, "lon": outer},
            device_id_type=MESH,
        )

    half = m // 4 * 4
    partner = lax.rem(m + 4, MEM)
    partner_half = 4 - half
    mates = [half + lax.rem(m + step, 4) for step in range(1, 4)]
    partner_mates = [partner_half + lax.rem(m + step, 4) for step in range(1, 4)]

    @pl.when(far)
    def _():
        for step in range(MEM):
            to = lax.rem(m + step, MEM)
            outward(m, to, to).start()

    def pass_on(block):
        across(block).start()

        @pl.when(jnp.logical_not(far))
        def _():
            outward(block, block, m).start()

    along(m, 3, partner).start()
    for n in range(3):
        along(m, n, mates[n]).start()
    pass_on(m)
    for step in range(1, MEM):
        end_copy(lax.rem(m + step, MEM), m).start()
    for n in range(3):
        arrival(1, mates[n]).wait_recv()
        pass_on(mates[n])
    arrival(1, partner).wait_recv()
    for n in range(3):
        along(partner, 4 + n, mates[n]).start()
    pass_on(partner)
    for n in range(3):
        arrival(1, partner_mates[n]).wait_recv()
        pass_on(partner_mates[n])

    @pl.when(jnp.logical_not(busy))
    def _():
        for step in range(1, MEM):
            row_copy(lax.rem(m + step, MEM), m).start()

    for copy in stat_copies:
        copy.wait()
    loads[-1].wait()
    fill(1, blocks, stats, flat, table)
    for block in range(MEM):
        arrival(theirs, block).wait_recv()
    fill(theirs, blocks, stats, flat, table)
    for block in range(MEM):
        arrival(mine, block).wait_recv()
    fill(mine, blocks, stats, flat, table)
    @pl.when(busy)
    def _():
        for step in LATE:
            row_copy(lax.rem(m + step, MEM), m).start()

    pieces = weigh(list_ref, table, picked, placing, stage, diagonal)

    for step in range(1, MEM):
        other = lax.rem(m + step, MEM)
        row_copy(other, other).wait_recv()
        end_copy(other, other).wait_recv()
    apply(pieces, states, edges, unpack, columns, done, out)

    for copy in edge_copies:
        copy.wait_send()
    for block in range(MEM):
        across(block).wait_send()
        outward(block, block, m).wait_send()
    along(m, 3, partner).wait_send()
    for n in range(3):
        along(m, n, mates[n]).wait_send()
        along(partner, 4 + n, mates[n]).wait_send()
    for step in range(1, MEM):
        other = lax.rem(m + step, MEM)
        row_copy(other, other).wait_send()
        end_copy(other, other).wait_send()


def exchange(lat, weights, bias, cell, value, weight, lists):
    hbm = pl.BlockSpec(memory_space=pltpu.HBM)
    vmem = pl.BlockSpec(memory_space=pltpu.VMEM)
    dma = pltpu.SemaphoreType.DMA
    return pl.pallas_call(
        exchange_kernel,
        out_shape=jax.ShapeDtypeStruct((MEMBERS * WIDTH, CHANS), F32),
        in_specs=[hbm] * 7,
        out_specs=vmem,
        scratch_shapes=[
            pltpu.VMEM(lat.shape, BF16),
            pltpu.VMEM(weights.shape, BF16),
            pltpu.VMEM(bias.shape, F32),
            pltpu.VMEM(cell.shape, jnp.int32),
            pltpu.SMEM(lists.shape, jnp.int32),
            pltpu.VMEM((3, MEM, OWN * 16, LANES), BF16),
            pltpu.VMEM((3, 2, 16, LANES), F32),
            pltpu.VMEM((MEM, SLOT, SETS * WIDE), BF16),
            pltpu.VMEM((MEM, 16, LANES), BF16),
            pltpu.VMEM((OWN, BAND, LANES), F32),
            pltpu.VMEM((OWN, BAND, LANES), F32),
            pltpu.VMEM((LANES, LANES), F32),
            pltpu.VMEM((PACK, 4 * LANES, 3 * WIDE), BF16),
            pltpu.VMEM((SETS, BAND, WIDE), F32),
            pltpu.VMEM((2 * SETS, BAND, LANES), F32),
            pltpu.VMEM((SETS * WIDE, BAND), BF16),
            pltpu.VMEM((SETS * WIDE, LANES), BF16),
            pltpu.VMEM((16, LANES), jnp.int32),
            pltpu.VMEM((16, LANES), jnp.int32),
            pltpu.VMEM((OWN * 16, LANES), F32),
            pltpu.VMEM((2, OWN * LAT, LANES), BF16),
            pltpu.VMEM((2, OWN * LAT, LANES), BF16),
            pltpu.VMEM((LAT, SLOT, SETS * WIDE), BF16),
            pltpu.VMEM((LAT * 16, LANES), F32),
            pltpu.VMEM((LAT, 16, LANES), BF16),
            pltpu.VMEM((MEM * OWN * 16, LANES), F32),
            pltpu.VMEM((3 * OBS, LANES), F32),
            pltpu.VMEM((GROUP, GROUPS * OBS_COL, LANES), F32),
            pltpu.VMEM((GROUP * LANES, 4 * WIDE), BF16),
            pltpu.VMEM((GROUPS * OBS_COL, 4 * WIDE), F32),
            pltpu.VMEM((SLOT * MEMBERS, LANES), F32),
            pltpu.VMEM((WIDE, WIDE), BF16),
            pltpu.VMEM((WIDE, PACK * LANES), BF16),
            pltpu.VMEM((MEMBERS * WIDTH, LANES), F32),
            dma((7,)),
            dma((2,)),
            dma((2,)),
            dma((2,)),
            dma((2,)),
            dma((7,)),
            dma((MEM,)),
            dma((MEM,)),
            dma((3, MEM)),
            dma((MEM,)),
            dma((MEM,)),
            dma((MEM,)),
            dma((MEM,)),
        ],
        compiler_params=pltpu.CompilerParams(
            collective_id=0, has_side_effects=True, vmem_limit_bytes=60 * 2**20
        ),
    )(lat, weights, bias, cell, value, weight, lists)


def local(latent, conv_weight, conv_bias, obs_cell, obs_value, obs_weight, obs_list):
    result = exchange(
        jnp.transpose(latent, (0, 2, 1, 3)),
        conv_weight,
        conv_bias.reshape(1, CHANS),
        obs_cell.reshape(16, LANES),
        obs_value.reshape(16, LANES),
        obs_weight.reshape(16, LANES),
        obs_list.reshape(WIDTH, 1, OBS_COL),
    )
    return jnp.transpose(result.reshape(MEMBERS, WIDTH, 1, CHANS), (0, 2, 1, 3))


def solution(mesh):
    placed = (
        P("mem", None, "lon", None),
        P(),
        P(),
        P("lon"),
        P("lon"),
        P("lon"),
        P("mem", "lon", None),
    )
    return jax.shard_map(
        local, mesh=mesh, in_specs=placed, out_specs=P(None, "mem", "lon", None), check_vma=False
    )
```

```python
import functools

import jax
import jax.numpy as jnp
from jax import lax
from jax.experimental import pallas as pl
from jax.experimental.pallas import tpu as pltpu
from jax.sharding import PartitionSpec as P

SWEEPS = 6
MEM = 8
MEMBERS = 48
CHANS = 78
WIDTH = 45
LAT = 8
OWN = 6
PACK = 3
SETS = OWN // PACK
OBS = 2048
OBS_COL = 64
LANES = 128
GROUP = 5
GROUPS = WIDTH // GROUP
CELLS = WIDTH * LAT
BAND = 384
WIDE = 2 * LANES
SLOT = 48
EARLY = (1, 2, 3, 5, 6, 7)
LATE = (4,)
F32 = jnp.float32
BF16 = jnp.bfloat16
MESH = pl.DeviceIdType.MESH


def dot(left, right):
    return jnp.dot(left, right, preferred_element_type=F32)


def silu(v):
    return v / (1.0 + jnp.exp(-v))


def split(v):
    high = v.astype(BF16)
    return high, (v - high.astype(F32)).astype(BF16)


def combine(parts):
    rows = parts.shape[0]
    cube = parts.reshape(rows // LAT, LAT, 3 * WIDE)
    spot = lax.broadcasted_iota(jnp.int32, (rows // LAT, LAT, WIDE), 1)
    above = pltpu.roll(cube[:, :, :WIDE], 1, 1)
    below = pltpu.roll(cube[:, :, 2 * WIDE :], LAT - 1, 1)
    total = cube[:, :, WIDE : 2 * WIDE]
    total = total + jnp.where(spot > 0, above, 0.0) + jnp.where(spot < LAT - 1, below, 0.0)
    return total.reshape(rows, WIDE)


def spread(piece):
    return jnp.concatenate([piece] * GROUP + [jnp.zeros((16, WIDE), BF16)], axis=0)


def build_constants(placing, diagonal, unpack):
    row = lax.broadcasted_iota(jnp.int32, (WIDE, WIDE), 0)
    col = lax.broadcasted_iota(jnp.int32, (WIDE, WIDE), 1)
    mask = jnp.zeros((WIDE, WIDE), F32)
    for s in range(GROUP):
        low, high = s * MEMBERS, (s + 1) * MEMBERS
        mask = jnp.where((row >= low) & (row < high) & (col >= low) & (col < high), 1.0, mask)
    diagonal[...] = mask.astype(BF16)
    row = lax.broadcasted_iota(jnp.int32, (WIDE, LANES), 0)
    col = lax.broadcasted_iota(jnp.int32, (WIDE, LANES), 1)
    for r in range(PACK):
        unpack[:, r * LANES : (r + 1) * LANES] = jnp.where(
            (row - CHANS * r == col) & (col < CHANS), 1.0, 0.0
        ).astype(BF16)
    row = lax.broadcasted_iota(jnp.int32, (LANES, WIDE), 0)
    col = lax.broadcasted_iota(jnp.int32, (LANES, WIDE), 1)
    member = row < MEMBERS
    for s in range(GROUP):
        inside = (col >= s * MEMBERS) & (col < (s + 1) * MEMBERS)
        same = col - s * MEMBERS == row
        kinds = (
            jnp.where(same, MEMBERS - 1.0, -1.0),
            jnp.where(member, -1.0, jnp.where((row == MEMBERS) | (row == MEMBERS + 2), MEMBERS, 0.0)),
            jnp.where((row == MEMBERS + 1) | (row == MEMBERS + 3), 1.0, 0.0),
        )
        for n, kind in enumerate(kinds):
            keep = inside & member if n == 0 else inside
            placing[s * LANES : (s + 1) * LANES, n * WIDE : (n + 1) * WIDE] = jnp.where(
                keep, kind, 0.0
            ).astype(BF16)


def fill(slot, blocks, stats, flat, table):
    flat[...] = blocks[slot].astype(F32).reshape(MEM * OWN * 16, LANES)
    blank = jnp.zeros((LANES - MEMBERS - 4, LANES), F32)

    def turn(k, carry):
        cells = flat[pl.ds(k, MEMBERS, stride=16), :]
        extra = [stats[slot, kind, pl.ds(k, 1), :] for kind in range(2)]
        high = [v.astype(BF16).astype(F32) for v in extra]
        low = [v - h for v, h in zip(extra, high)]
        whole = jnp.concatenate([cells] + high + low + [blank], axis=0)
        start = pl.multiple_of(slot * OBS + k * LANES, LANES)
        table[pl.ds(start, LANES), :] = whole.T
        return carry

    lax.fori_loop(0, 16, turn, 0, unroll=8)


def weigh(list_ref, table, picked, placing, stage, diagonal, between):
    def gather(q, carry):
        base = q * OBS_COL
        for s in range(GROUP):
            for o in range(OBS_COL):
                index = list_ref[q * GROUP + s, 0, o]
                picked[s, pl.ds(base + o, 1), :] = table[pl.ds(index, 1), :]
        return carry

    lax.fori_loop(0, GROUPS, gather, 0)
    between()
    found = jnp.concatenate([picked[s].astype(BF16) for s in range(GROUP)], axis=1)
    stage[...] = dot(found, placing[...])

    eye = jnp.zeros((MEMBERS, WIDE), F32)
    row48 = lax.broadcasted_iota(jnp.int32, (MEMBERS, WIDE), 0)
    col48 = lax.broadcasted_iota(jnp.int32, (MEMBERS, WIDE), 1)
    for s in range(GROUP):
        eye = jnp.where(col48 - MEMBERS * s == row48, 1.0, eye)
    lane = lax.broadcasted_iota(jnp.int32, (1, WIDE), 1)
    block48 = [(lane >= s * MEMBERS) & (lane < (s + 1) * MEMBERS) for s in range(GROUP)]
    every = range(GROUPS)

    def block_sum(pieces):
        return dot(jnp.concatenate(pieces, axis=0), diagonal[...])

    grams, proj, traces = [], [], []
    for q in every:
        rows = slice(q * OBS_COL, (q + 1) * OBS_COL)
        pert = stage[rows, :WIDE] * (1.0 / MEMBERS)
        depart = stage[rows, WIDE : 2 * WIDE] * (1.0 / MEMBERS)
        scaled = pert * stage[rows, 2 * WIDE :]
        proj.append(jnp.sum(scaled * depart, axis=0, keepdims=True))
        traces.append(jnp.sum(scaled * pert, axis=0, keepdims=True))
        high, low = split(pert)
        scaled_high, scaled_low = split(scaled)
        square = lax.dot_general(
            jnp.concatenate([scaled_high, scaled_low, scaled_high], axis=0),
            jnp.concatenate([high, high, low], axis=0),
            (((0,), (0,)), ((), ())),
            preferred_element_type=F32,
        )
        gram = (MEMBERS - 1.0) * eye
        for s in range(GROUP):
            piece = square[s * MEMBERS : (s + 1) * MEMBERS]
            gram = gram + jnp.where(block48[s], piece, 0.0)
        grams.append(gram)
    trace = jnp.concatenate(traces + [jnp.zeros((16 - GROUPS, WIDE), F32)], axis=0)
    one = trace.astype(BF16)
    two, three = split(trace - one.astype(F32))
    sums = block_sum([one, two, three])
    scales = MEMBERS * (MEMBERS - 1.0) + sums[:16] + sums[16:32] + sums[32:]
    invert, reroot = 1.0 / scales, lax.rsqrt(scales)

    def times(parts, high, low):
        count = len(parts)
        first = dot(jnp.concatenate([x for pair in parts for x in pair], axis=0), high)
        second = dot(jnp.concatenate([pair[0] for pair in parts], axis=0), low)
        size = parts[0][0].shape[0]
        return [
            first[2 * n * size : (2 * n + 1) * size]
            + first[(2 * n + 1) * size : (2 * n + 2) * size]
            + second[n * size : (n + 1) * size]
            for n in range(count)
        ]

    def lay(pair):
        return [spread(piece) * diagonal[...] for piece in pair]

    ratio = [grams[q] * invert[q : q + 1] for q in every]
    inverse = [None] * GROUPS
    for sweep in range(SWEEPS):
        factor = [1.5 * eye - 0.5 * r for r in ratio]
        weights = [lay(split(f)) for f in factor]
        products = []
        for q in every:
            todo = []
            if sweep < SWEEPS - 1:
                todo.append(split(ratio[q]))
            if sweep > 0:
                todo.append(split(inverse[q]))
            products.append(times(todo, *weights[q]))
        inverse = [products[q][-1] if sweep > 0 else factor[q] for q in every]
        if sweep < SWEEPS - 1:
            ratio = [times([split(products[q][0])], *weights[q])[0] for q in every]

    root = [inverse[q] * reroot[q : q + 1] for q in every]
    weights = [lay(split(r)) for r in root]
    vector = proj
    spot = lax.broadcasted_iota(jnp.int32, (16, WIDE), 0)
    for _ in range(2):
        rows = []
        for q in every:
            high = vector[q].astype(BF16).astype(F32)
            low = vector[q] - high
            rows.append(jnp.where(spot == 0, high, jnp.where(spot == 1, low, 0.0)).astype(BF16))
        first = [dot(rows[q], weights[q][0]) for q in every]
        second = [dot(rows[q], weights[q][1]) for q in every]
        vector = [first[q][0:1] + first[q][1:2] + second[q][0:1] for q in every]
    transform = [(MEMBERS - 1.0) ** 0.5 * root[q] + vector[q] for q in every]
    sums = block_sum([piece for t in transform for piece in split(t)])
    pieces = []
    for q in every:
        at = 2 * q * MEMBERS
        both = sums[at : at + MEMBERS] + sums[at + MEMBERS : at + 2 * MEMBERS]
        pieces.append(lay(split(transform[q] + (1.0 - both) * (1.0 / MEMBERS))))
    return pieces


def apply(pieces, states, edges, unpack, columns, out):
    for source in range(MEM):
        for g in range(SETS):
            parts = dot(states[source, :, g * WIDE : (g + 1) * WIDE], unpack[...])
            for r in range(PACK):
                columns[pl.ds(source * OWN + g * PACK + r, SLOT, stride=MEMBERS), :] = parts[
                    :, r * LANES : (r + 1) * LANES
                ]
    ends = edges[...].astype(F32)
    for g in range(SETS):
        sides = [
            jnp.concatenate([ends[:, 4 * g + side, :], ends[:, 4 * g + 2 + side, :]], axis=1)
            for side in range(2)
        ]
        parts = dot(jnp.concatenate(sides, axis=0).astype(BF16), unpack[...])
        for side, column in ((0, 0), (1, WIDTH - 1)):
            for r in range(PACK):
                columns[pl.ds(column * MEMBERS + g * PACK + r, MEM, stride=OWN), :] = parts[
                    side * MEM : (side + 1) * MEM, r * LANES : (r + 1) * LANES
                ]

    for q in range(GROUPS):
        field = columns[q * GROUP * MEMBERS : q * GROUP * MEMBERS + WIDE, :].astype(BF16)
        both = dot(jnp.concatenate(pieces[q], axis=0), field)
        result = both[:WIDE] + both[WIDE:]
        for s in range(GROUP):
            out[pl.ds(q * GROUP + s, MEMBERS, stride=WIDTH), :] = result[
                s * MEMBERS : (s + 1) * MEMBERS
            ]


def exchange_kernel(
    lat_hbm, w_hbm, bias_hbm, cell_hbm, value_hbm, weight_hbm, list_hbm,
    out,
    lat_ref, w_ref, bias_ref, cell_ref, list_ref, blocks, stats, states, edges,
    field, act, wpad, taps, total, halves, turned, turned_rim, cellp, cellc,
    own, edge_out, edge_in, rows_out, ends, ends_out,
    flat, table, picked, placing, stage, columns, diagonal, unpack,
    loaded, edge_sent, edge_got, stat_sent, stat_got, mate_sent, sib_sent, outer_sent, block_got,
    state_sent, state_got, end_sent, end_got,
):
    m = lax.axis_index("mem")
    t = lax.axis_index("lon")
    tiles = lax.axis_size("lon")
    core = lax.rem(t, 2)
    left = lax.rem(t + tiles - 1, tiles)
    right = lax.rem(t + 1, tiles)
    outer = jnp.where(core == 0, left, right)
    inner = jnp.where(core == 0, right, left)
    mine, theirs = 2 * core, 2 - 2 * core
    far = lax.rem(jnp.where(core == 0, t, t + 1), tiles // 2) == 0

    quarter, pair = tiles // 4, lax.rem(t // 2, tiles // 4)
    busy = (pair == 0) | (pair == quarter - 1)

    barrier = pltpu.get_barrier_semaphore()
    for lon in (left, right):
        pl.semaphore_signal(barrier, inc=1, device_id={"lon": lon}, device_id_type=MESH)

    @pl.when(far)
    def _():
        for step in range(1, MEM):
            to = {"mem": lax.rem(m + step, MEM), "lon": outer}
            pl.semaphore_signal(barrier, inc=1, device_id=to, device_id_type=MESH)

    for step in range(1, MEM):
        to = {"mem": lax.rem(m + step, MEM)}
        pl.semaphore_signal(barrier, inc=1, device_id=to, device_id_type=MESH)

    loads = [
        pltpu.make_async_copy(source, target, loaded.at[n])
        for n, (source, target) in enumerate(
            (
                (lat_hbm, lat_ref),
                (w_hbm, w_ref),
                (bias_hbm, bias_ref),
                (cell_hbm, cell_ref),
                (value_hbm, stats.at[1, 0]),
                (weight_hbm, stats.at[1, 1]),
                (list_hbm, list_ref),
            )
        )
    ]
    for load in loads:
        load.start()

    edge_out[...] = jnp.zeros_like(edge_out)
    field[...] = jnp.zeros_like(field)
    wpad[...] = jnp.zeros_like(wpad)
    ends[...] = jnp.zeros_like(ends)
    loads[0].wait()
    for side, column in ((0, WIDTH - 1), (1, 0)):
        edge = lat_ref[:, column].astype(F32).reshape(OWN * LAT, CHANS)
        edge_out[side, :, :CHANS] = edge.astype(BF16)

    for k in range(OWN):
        field[k, LAT : LAT + CELLS, :CHANS] = lat_ref[k].astype(F32).reshape(CELLS, CHANS)
    act[...] = silu(field[...])

    for load in loads[1:-1]:
        load.wait()
    lane = lax.broadcasted_iota(jnp.int32, (LANES, WIDE), 1)
    depth = lax.broadcasted_iota(jnp.int32, (LANES, WIDE), 0)
    blank = jnp.zeros((LANES, LANES), F32)
    for a in range(3):
        for b in range(3):
            wpad[:CHANS, :CHANS] = w_ref[a, b].astype(F32)
            whole = jnp.concatenate([wpad[...], blank], axis=1)
            for r in range(PACK):
                moved = whole if r == 0 else pltpu.roll(whole, CHANS * r, 1)
                taps[r, b * LANES : (b + 1) * LANES, a * WIDE : (a + 1) * WIDE] = moved.astype(BF16)
    for r in range(PACK):
        same = jnp.where((lane - CHANS * r == depth) & (depth < CHANS), 1.0, 0.0)
        taps[r, 3 * LANES :, :WIDE] = jnp.zeros((LANES, WIDE), BF16)
        taps[r, 3 * LANES :, WIDE : 2 * WIDE] = same.astype(BF16)
        taps[r, 3 * LANES :, 2 * WIDE :] = jnp.zeros((LANES, WIDE), BF16)
    wpad[:1, :CHANS] = bias_ref[...]
    bias = jnp.concatenate([wpad[:8, :], blank[:8, :]], axis=1)
    bias = bias + pltpu.roll(bias, CHANS, 1) + pltpu.roll(bias, 2 * CHANS, 1)
    bias = jnp.where(lane[:8, :] < PACK * CHANS, bias, 0.0)[:1, :]

    span = CELLS + LAT
    for g in range(SETS):
        parts = None
        for r in range(PACK):
            k = PACK * g + r
            sides = [act[k, LAT * b : LAT * b + span, :].astype(BF16) for b in range(3)]
            sides.append(field[k, LAT : LAT + span, :].astype(BF16))
            part = dot(jnp.concatenate(sides, axis=1), taps[r])
            parts = part if parts is None else parts + part
        summed = combine(parts) + bias
        total[g, :span] = summed
        total[g, span:] = jnp.zeros((BAND - span, WIDE), F32)
        for h in range(2):
            halves[2 * g + h] = total[g, :, h * LANES : (h + 1) * LANES]

    named = cell_ref[...]
    pixel = jnp.floor((named.astype(F32) + 0.5) * (1.0 / CHANS)).astype(jnp.int32)
    row = jnp.floor((pixel.astype(F32) + 0.5) * (1.0 / WIDTH)).astype(jnp.int32)
    cellc[...] = named - CHANS * pixel
    cellp[...] = (pixel - WIDTH * row) * LAT + row

    pl.semaphore_wait(barrier, jnp.where(far, 2 * MEM, MEM + 1))

    edge_copies = [
        pltpu.make_async_remote_copy(
            src_ref=edge_out.at[side],
            dst_ref=edge_in.at[side],
            send_sem=edge_sent.at[side],
            recv_sem=edge_got.at[side],
            device_id={"lon": lon},
            device_id_type=MESH,
        )
        for side, lon in ((0, right), (1, left))
    ]
    stat_copies = [
        pltpu.make_async_remote_copy(
            src_ref=stats.at[1],
            dst_ref=stats.at[2 * side],
            send_sem=stat_sent.at[side],
            recv_sem=stat_got.at[side],
            device_id={"lon": lon},
            device_id_type=MESH,
        )
        for side, lon in ((0, right), (1, left))
    ]
    for copy in edge_copies:
        copy.start()


    def mend(side):
        pltpu.make_async_remote_copy(
            src_ref=edge_out.at[side],
            dst_ref=edge_in.at[side],
            send_sem=edge_sent.at[side],
            recv_sem=edge_got.at[side],
            device_id={"lon": inner},
            device_id_type=MESH,
        ).wait_recv()
        turn = silu(edge_in[side].astype(F32)).astype(BF16).astype(F32)
        tap = pl.multiple_of(2 * side * LANES, LANES)
        parts = None
        for r in range(PACK):
            pick = [turn[(PACK * g + r) * LAT : (PACK * g + r + 1) * LAT] for g in range(SETS)]
            part = dot(jnp.concatenate(pick, axis=0).astype(BF16), taps[r, pl.ds(tap, LANES)])
            parts = part if parts is None else parts + part
        extra = combine(parts)
        first = pl.multiple_of(side * (CELLS - LAT), LAT)
        for g in range(SETS):
            edge = total[g, pl.ds(first, LAT)] + extra[g * LAT : (g + 1) * LAT]
            total[g, pl.ds(first, LAT)] = edge
            for h in range(2):
                ends[pl.ds(4 * g + 2 * h + side, LAT, stride=16), :] = edge[
                    :, h * LANES : (h + 1) * LANES
                ]

    for i in range(LAT):
        for half in range(2 * SETS):
            rows_out[i, :, half * LANES : (half + 1) * LANES] = halves[
                half, pl.ds(i, SLOT, stride=LAT), :
            ].astype(BF16)
    states[m] = rows_out[m]

    def row_copy(to, source):
        return pltpu.make_async_remote_copy(
            src_ref=rows_out.at[to],
            dst_ref=states.at[source],
            send_sem=state_sent.at[to],
            recv_sem=state_got.at[source],
            device_id={"mem": to},
            device_id_type=MESH,
        )

    def end_copy(to, source):
        return pltpu.make_async_remote_copy(
            src_ref=ends_out.at[to],
            dst_ref=edges.at[source],
            send_sem=end_sent.at[to],
            recv_sem=end_got.at[source],
            device_id={"mem": to},
            device_id_type=MESH,
        )


    @pl.when(busy)
    def _():
        for step in EARLY:
            row_copy(lax.rem(m + step, MEM), m).start()

    build_constants(placing, diagonal, unpack)
    channel = lax.broadcasted_iota(jnp.int32, (WIDE, WIDE), 0)
    rim = pl.multiple_of(jnp.where(core == 0, 0, CELLS - LAT), LAT)

    def choose_from(source, first_cell, more):
        place = lax.broadcasted_iota(jnp.int32, (source.shape[1], LANES), 0) + first_cell

        def choose(pair, carry):
            rows = [pl.ds(2 * pair + n, 1) for n in range(2)]
            hot = jnp.concatenate(
                [jnp.where(place == cellp[at, :], 1.0, 0.0).astype(BF16) for at in rows], axis=1
            )
            chans = jnp.concatenate([cellc[at, :] for at in rows], axis=1)
            for g in range(SETS):
                cells = dot(source[g * WIDE : (g + 1) * WIDE, :], hot)
                for r in range(PACK):
                    low, high = CHANS * r // 8 * 8, -(-CHANS * (r + 1) // 8) * 8
                    mask = channel[low:high] - CHANS * r == chans
                    found = jnp.sum(jnp.where(mask, cells[low:high], 0.0), axis=0, keepdims=True)
                    for n in range(2):
                        spot = pl.ds((PACK * g + r) * 16 + 2 * pair + n, 1)
                        piece = found[:, n * LANES : (n + 1) * LANES]
                        own[spot, :] = own[spot, :] + piece if more else piece
            return carry

        lax.fori_loop(0, OBS // WIDE, choose, 0, unroll=2)

    mend(1 - core)
    cell_row = lax.broadcasted_iota(jnp.int32, (BAND, WIDE), 0)
    for g in range(SETS):
        keep = (cell_row < rim) | (cell_row >= rim + LAT)
        turned[g * WIDE : (g + 1) * WIDE] = jnp.where(keep, total[g], 0.0).T.astype(BF16)
    choose_from(turned, 0, False)

    mend(core)
    for copy in stat_copies:
        copy.start()
    ends_out[...] = ends[...].astype(BF16).reshape(LAT, 16, LANES)
    edges[m] = ends_out[m]
    for g in range(SETS):
        edge = jnp.concatenate(
            [total[g, pl.ds(rim, LAT), :], jnp.zeros((LANES - LAT, WIDE), F32)], axis=0
        )
        turned_rim[g * WIDE : (g + 1) * WIDE] = edge.T.astype(BF16)
    choose_from(turned_rim, rim, True)
    blocks[1, m] = own[...].astype(BF16)

    def arrival(slot, block):
        return pltpu.make_async_remote_copy(
            src_ref=blocks.at[1, block],
            dst_ref=blocks.at[slot, block],
            send_sem=sib_sent.at[block],
            recv_sem=block_got.at[slot, block],
            device_id={"lon": inner},
            device_id_type=MESH,
        )

    def along(block, sent, to):
        return pltpu.make_async_remote_copy(
            src_ref=blocks.at[1, block],
            dst_ref=blocks.at[1, block],
            send_sem=mate_sent.at[sent],
            recv_sem=block_got.at[1, block],
            device_id={"mem": to},
            device_id_type=MESH,
        )

    def across(block):
        return pltpu.make_async_remote_copy(
            src_ref=blocks.at[1, block],
            dst_ref=blocks.at[mine, block],
            send_sem=sib_sent.at[block],
            recv_sem=block_got.at[mine, block],
            device_id={"lon": inner},
            device_id_type=MESH,
        )

    def outward(block, sent, to):
        return pltpu.make_async_remote_copy(
            src_ref=blocks.at[1, block],
            dst_ref=blocks.at[theirs, block],
            send_sem=outer_sent.at[sent],
            recv_sem=block_got.at[theirs, block],
            device_id={"mem": to, "lon": outer},
            device_id_type=MESH,
        )

    half = m // 4 * 4
    partner = lax.rem(m + 4, MEM)
    partner_half = 4 - half
    mates = [half + lax.rem(m + step, 4) for step in range(1, 4)]
    partner_mates = [partner_half + lax.rem(m + step, 4) for step in range(1, 4)]

    @pl.when(far)
    def _():
        for step in range(1, MEM, 2):
            to = lax.rem(m + step, MEM)
            outward(m, to, to).start()

    def pass_on(block):
        across(block).start()

        @pl.when(jnp.logical_not(far))
        def _():
            outward(block, block, m).start()

    along(m, 3, partner).start()
    for n in range(3):
        along(m, n, mates[n]).start()
    pass_on(m)
    for step in range(1, MEM):
        end_copy(lax.rem(m + step, MEM), m).start()
    for n in range(3):
        arrival(1, mates[n]).wait_recv()
        pass_on(mates[n])
    arrival(1, partner).wait_recv()
    for n in range(3):
        along(partner, 4 + n, mates[n]).start()
    pass_on(partner)
    for n in range(3):
        arrival(1, partner_mates[n]).wait_recv()
        pass_on(partner_mates[n])

    @pl.when(jnp.logical_not(busy))
    def _():
        for step in range(1, MEM):
            row_copy(lax.rem(m + step, MEM), m).start()

    beside = m + 1 - 2 * lax.rem(m, 2)

    def hand(block, sent):
        return pltpu.make_async_remote_copy(
            src_ref=blocks.at[mine, block],
            dst_ref=blocks.at[mine, block],
            send_sem=outer_sent.at[sent],
            recv_sem=block_got.at[mine, block],
            device_id={"mem": beside},
            device_id_type=MESH,
        )

    @pl.when(far)
    def _():
        for step in range(1, MEM, 2):
            block = lax.rem(m + step, MEM)
            arrival(mine, block).wait_recv()
            hand(block, lax.rem(m + step - 1, MEM)).start()

    for copy in stat_copies:
        copy.wait()
    loads[-1].wait()
    fill(1, blocks, stats, flat, table)
    for block in range(MEM):
        arrival(theirs, block).wait_recv()
    fill(theirs, blocks, stats, flat, table)
    @pl.when(far)
    def _():
        for step in range(0, MEM, 2):
            arrival(mine, lax.rem(m + step, MEM)).wait_recv()

    @pl.when(jnp.logical_not(far))
    def _():
        for block in range(MEM):
            arrival(mine, block).wait_recv()

    fill(mine, blocks, stats, flat, table)
    def send_late():
        @pl.when(busy)
        def _():
            for step in LATE:
                row_copy(lax.rem(m + step, MEM), m).start()

    pieces = weigh(list_ref, table, picked, placing, stage, diagonal, send_late)

    for step in range(1, MEM):
        other = lax.rem(m + step, MEM)
        row_copy(other, other).wait_recv()
        end_copy(other, other).wait_recv()
    apply(pieces, states, edges, unpack, columns, out)

    for copy in edge_copies:
        copy.wait_send()
    for block in range(MEM):
        across(block).wait_send()
        outward(block, block, m).wait_send()
    along(m, 3, partner).wait_send()
    for n in range(3):
        along(m, n, mates[n]).wait_send()
        along(partner, 4 + n, mates[n]).wait_send()
    for step in range(1, MEM):
        other = lax.rem(m + step, MEM)
        row_copy(other, other).wait_send()
        end_copy(other, other).wait_send()


def exchange(lat, weights, bias, cell, value, weight, lists):
    hbm = pl.BlockSpec(memory_space=pltpu.HBM)
    vmem = pl.BlockSpec(memory_space=pltpu.VMEM)
    dma = pltpu.SemaphoreType.DMA
    return pl.pallas_call(
        exchange_kernel,
        out_shape=jax.ShapeDtypeStruct((MEMBERS * WIDTH, LANES), F32),
        in_specs=[hbm] * 7,
        out_specs=vmem,
        scratch_shapes=[
            pltpu.VMEM(lat.shape, BF16),
            pltpu.VMEM(weights.shape, BF16),
            pltpu.VMEM(bias.shape, F32),
            pltpu.VMEM(cell.shape, jnp.int32),
            pltpu.SMEM(lists.shape, jnp.int32),
            pltpu.VMEM((3, MEM, OWN * 16, LANES), BF16),
            pltpu.VMEM((3, 2, 16, LANES), F32),
            pltpu.VMEM((MEM, SLOT, SETS * WIDE), BF16),
            pltpu.VMEM((MEM, 16, LANES), BF16),
            pltpu.VMEM((OWN, BAND, LANES), F32),
            pltpu.VMEM((OWN, BAND, LANES), F32),
            pltpu.VMEM((LANES, LANES), F32),
            pltpu.VMEM((PACK, 4 * LANES, 3 * WIDE), BF16),
            pltpu.VMEM((SETS, BAND, WIDE), F32),
            pltpu.VMEM((2 * SETS, BAND, LANES), F32),
            pltpu.VMEM((SETS * WIDE, BAND), BF16),
            pltpu.VMEM((SETS * WIDE, LANES), BF16),
            pltpu.VMEM((16, LANES), jnp.int32),
            pltpu.VMEM((16, LANES), jnp.int32),
            pltpu.VMEM((OWN * 16, LANES), F32),
            pltpu.VMEM((2, OWN * LAT, LANES), BF16),
            pltpu.VMEM((2, OWN * LAT, LANES), BF16),
            pltpu.VMEM((LAT, SLOT, SETS * WIDE), BF16),
            pltpu.VMEM((LAT * 16, LANES), F32),
            pltpu.VMEM((LAT, 16, LANES), BF16),
            pltpu.VMEM((MEM * OWN * 16, LANES), F32),
            pltpu.VMEM((3 * OBS, LANES), F32),
            pltpu.VMEM((GROUP, GROUPS * OBS_COL, LANES), F32),
            pltpu.VMEM((GROUP * LANES, 3 * WIDE), BF16),
            pltpu.VMEM((GROUPS * OBS_COL, 3 * WIDE), F32),
            pltpu.VMEM((SLOT * MEMBERS, LANES), F32),
            pltpu.VMEM((WIDE, WIDE), BF16),
            pltpu.VMEM((WIDE, PACK * LANES), BF16),
            dma((7,)),
            dma((2,)),
            dma((2,)),
            dma((2,)),
            dma((2,)),
            dma((7,)),
            dma((MEM,)),
            dma((MEM,)),
            dma((3, MEM)),
            dma((MEM,)),
            dma((MEM,)),
            dma((MEM,)),
            dma((MEM,)),
        ],
        compiler_params=pltpu.CompilerParams(
            collective_id=0, has_side_effects=True, vmem_limit_bytes=60 * 2**20
        ),
    )(lat, weights, bias, cell, value, weight, lists)


def local(latent, conv_weight, conv_bias, obs_cell, obs_value, obs_weight, obs_list):
    result = exchange(
        jnp.transpose(latent, (0, 2, 1, 3)),
        conv_weight,
        conv_bias.reshape(1, CHANS),
        obs_cell.reshape(16, LANES),
        obs_value.reshape(16, LANES),
        obs_weight.reshape(16, LANES),
        obs_list.reshape(WIDTH, 1, OBS_COL),
    )
    return jnp.transpose(result[:, :CHANS].reshape(MEMBERS, WIDTH, 1, CHANS), (0, 2, 1, 3))


def solution(mesh):
    placed = (
        P("mem", None, "lon", None),
        P(),
        P(),
        P("lon"),
        P("lon"),
        P("lon"),
        P("mem", "lon", None),
    )
    return jax.shard_map(
        local, mesh=mesh, in_specs=placed, out_specs=P(None, "mem", "lon", None), check_vma=False
    )
```

```python
import functools

import jax
import jax.numpy as jnp
from jax import lax
from jax.experimental import pallas as pl
from jax.experimental.pallas import tpu as pltpu
from jax.sharding import PartitionSpec as P

SWEEPS = 6
MEM = 8
MEMBERS = 48
CHANS = 78
WIDTH = 45
LAT = 8
OWN = 6
PACK = 3
SETS = OWN // PACK
OBS = 2048
OBS_COL = 64
LANES = 128
GROUP = 5
GROUPS = WIDTH // GROUP
CELLS = WIDTH * LAT
BAND = 384
WIDE = 2 * LANES
SLOT = 48
EARLY = (1, 2, 3, 5, 6, 7)
LATE = (4,)
F32 = jnp.float32
BF16 = jnp.bfloat16
MESH = pl.DeviceIdType.MESH


def dot(left, right):
    return jnp.dot(left, right, preferred_element_type=F32)


def silu(v):
    return v / (1.0 + jnp.exp(-v))


def split(v):
    high = v.astype(BF16)
    return high, (v - high.astype(F32)).astype(BF16)


def combine(parts):
    rows = parts.shape[0]
    cube = parts.reshape(rows // LAT, LAT, 3 * WIDE)
    spot = lax.broadcasted_iota(jnp.int32, (rows // LAT, LAT, WIDE), 1)
    above = pltpu.roll(cube[:, :, :WIDE], 1, 1)
    below = pltpu.roll(cube[:, :, 2 * WIDE :], LAT - 1, 1)
    total = cube[:, :, WIDE : 2 * WIDE]
    total = total + jnp.where(spot > 0, above, 0.0) + jnp.where(spot < LAT - 1, below, 0.0)
    return total.reshape(rows, WIDE)


def spread(piece):
    return jnp.concatenate([piece] * GROUP + [jnp.zeros((16, WIDE), BF16)], axis=0)


def build_constants(placing, diagonal, unpack):
    row = lax.broadcasted_iota(jnp.int32, (WIDE, WIDE), 0)
    col = lax.broadcasted_iota(jnp.int32, (WIDE, WIDE), 1)
    mask = jnp.zeros((WIDE, WIDE), F32)
    for s in range(GROUP):
        low, high = s * MEMBERS, (s + 1) * MEMBERS
        mask = jnp.where((row >= low) & (row < high) & (col >= low) & (col < high), 1.0, mask)
    diagonal[...] = mask.astype(BF16)
    row = lax.broadcasted_iota(jnp.int32, (WIDE, LANES), 0)
    col = lax.broadcasted_iota(jnp.int32, (WIDE, LANES), 1)
    for r in range(PACK):
        unpack[:, r * LANES : (r + 1) * LANES] = jnp.where(
            (row - CHANS * r == col) & (col < CHANS), 1.0, 0.0
        ).astype(BF16)
    row = lax.broadcasted_iota(jnp.int32, (LANES, WIDE), 0)
    col = lax.broadcasted_iota(jnp.int32, (LANES, WIDE), 1)
    member = row < MEMBERS
    for s in range(GROUP):
        inside = (col >= s * MEMBERS) & (col < (s + 1) * MEMBERS)
        same = col - s * MEMBERS == row
        kinds = (
            jnp.where(same, MEMBERS - 1.0, -1.0),
            jnp.where(member, -1.0, jnp.where((row == MEMBERS) | (row == MEMBERS + 2), MEMBERS, 0.0)),
            jnp.where((row == MEMBERS + 1) | (row == MEMBERS + 3), 1.0, 0.0),
        )
        for n, kind in enumerate(kinds):
            keep = inside & member if n == 0 else inside
            placing[s * LANES : (s + 1) * LANES, n * WIDE : (n + 1) * WIDE] = jnp.where(
                keep, kind, 0.0
            ).astype(BF16)


def fill(slot, blocks, stats, flat, table):
    flat[...] = blocks[slot].astype(F32).reshape(MEM * OWN * 16, LANES)
    blank = jnp.zeros((LANES - MEMBERS - 4, LANES), F32)

    def turn(k, carry):
        cells = flat[pl.ds(k, MEMBERS, stride=16), :]
        extra = [stats[slot, kind, pl.ds(k, 1), :] for kind in range(2)]
        high = [v.astype(BF16).astype(F32) for v in extra]
        low = [v - h for v, h in zip(extra, high)]
        whole = jnp.concatenate([cells] + high + low + [blank], axis=0)
        start = pl.multiple_of(slot * OBS + k * LANES, LANES)
        table[pl.ds(start, LANES), :] = whole.T
        return carry

    lax.fori_loop(0, 16, turn, 0, unroll=8)


def weigh(list_ref, table, picked, placing, stage, diagonal, between):
    def gather(q, carry):
        base = q * OBS_COL
        for s in range(GROUP):
            for o in range(OBS_COL):
                index = list_ref[q * GROUP + s, 0, o]
                picked[s, pl.ds(base + o, 1), :] = table[pl.ds(index, 1), :]
        return carry

    lax.fori_loop(0, GROUPS, gather, 0)
    between()
    found = jnp.concatenate([picked[s].astype(BF16) for s in range(GROUP)], axis=1)
    stage[...] = dot(found, placing[...])

    eye = jnp.zeros((MEMBERS, WIDE), F32)
    row48 = lax.broadcasted_iota(jnp.int32, (MEMBERS, WIDE), 0)
    col48 = lax.broadcasted_iota(jnp.int32, (MEMBERS, WIDE), 1)
    for s in range(GROUP):
        eye = jnp.where(col48 - MEMBERS * s == row48, 1.0, eye)
    lane = lax.broadcasted_iota(jnp.int32, (1, WIDE), 1)
    block48 = [(lane >= s * MEMBERS) & (lane < (s + 1) * MEMBERS) for s in range(GROUP)]
    every = range(GROUPS)

    def block_sum(pieces):
        return dot(jnp.concatenate(pieces, axis=0), diagonal[...])

    grams, proj, traces = [], [], []
    for q in every:
        rows = slice(q * OBS_COL, (q + 1) * OBS_COL)
        pert = stage[rows, :WIDE] * (1.0 / MEMBERS)
        depart = stage[rows, WIDE : 2 * WIDE] * (1.0 / MEMBERS)
        scaled = pert * stage[rows, 2 * WIDE :]
        proj.append(jnp.sum(scaled * depart, axis=0, keepdims=True))
        traces.append(jnp.sum(scaled * pert, axis=0, keepdims=True))
        high, low = split(pert)
        scaled_high, scaled_low = split(scaled)
        square = lax.dot_general(
            jnp.concatenate([scaled_high, scaled_low, scaled_high], axis=0),
            jnp.concatenate([high, high, low], axis=0),
            (((0,), (0,)), ((), ())),
            preferred_element_type=F32,
        )
        gram = (MEMBERS - 1.0) * eye
        for s in range(GROUP):
            piece = square[s * MEMBERS : (s + 1) * MEMBERS]
            gram = gram + jnp.where(block48[s], piece, 0.0)
        grams.append(gram)
    trace = jnp.concatenate(traces + [jnp.zeros((16 - GROUPS, WIDE), F32)], axis=0)
    one = trace.astype(BF16)
    two, three = split(trace - one.astype(F32))
    sums = block_sum([one, two, three])
    scales = MEMBERS * (MEMBERS - 1.0) + sums[:16] + sums[16:32] + sums[32:]
    invert, reroot = 1.0 / scales, lax.rsqrt(scales)

    def times(parts, high, low):
        count = len(parts)
        first = dot(jnp.concatenate([x for pair in parts for x in pair], axis=0), high)
        second = dot(jnp.concatenate([pair[0] for pair in parts], axis=0), low)
        size = parts[0][0].shape[0]
        return [
            first[2 * n * size : (2 * n + 1) * size]
            + first[(2 * n + 1) * size : (2 * n + 2) * size]
            + second[n * size : (n + 1) * size]
            for n in range(count)
        ]

    def lay(pair):
        return [spread(piece) * diagonal[...] for piece in pair]

    ratio = [grams[q] * invert[q : q + 1] for q in every]
    inverse = [None] * GROUPS
    for sweep in range(SWEEPS):
        factor = [1.5 * eye - 0.5 * r for r in ratio]
        weights = [lay(split(f)) for f in factor]
        products = []
        for q in every:
            todo = []
            if sweep < SWEEPS - 1:
                todo.append(split(ratio[q]))
            if sweep > 0:
                todo.append(split(inverse[q]))
            products.append(times(todo, *weights[q]))
        inverse = [products[q][-1] if sweep > 0 else factor[q] for q in every]
        if sweep < SWEEPS - 1:
            ratio = [times([split(products[q][0])], *weights[q])[0] for q in every]

    root = [inverse[q] * reroot[q : q + 1] for q in every]
    weights = [lay(split(r)) for r in root]
    vector = proj
    spot = lax.broadcasted_iota(jnp.int32, (16, WIDE), 0)
    for _ in range(2):
        rows = []
        for q in every:
            high = vector[q].astype(BF16).astype(F32)
            low = vector[q] - high
            rows.append(jnp.where(spot == 0, high, jnp.where(spot == 1, low, 0.0)).astype(BF16))
        first = [dot(rows[q], weights[q][0]) for q in every]
        second = [dot(rows[q], weights[q][1]) for q in every]
        vector = [first[q][0:1] + first[q][1:2] + second[q][0:1] for q in every]
    transform = [(MEMBERS - 1.0) ** 0.5 * root[q] + vector[q] for q in every]
    sums = block_sum([piece for t in transform for piece in split(t)])
    pieces = []
    for q in every:
        at = 2 * q * MEMBERS
        both = sums[at : at + MEMBERS] + sums[at + MEMBERS : at + 2 * MEMBERS]
        pieces.append(lay(split(transform[q] + (1.0 - both) * (1.0 / MEMBERS))))
    return pieces


def apply(pieces, states, edges, unpack, columns, out):
    for source in range(MEM):
        for g in range(SETS):
            parts = dot(states[source, :, g * WIDE : (g + 1) * WIDE], unpack[...])
            for r in range(PACK):
                columns[pl.ds(source * OWN + g * PACK + r, SLOT, stride=MEMBERS), :] = parts[
                    :, r * LANES : (r + 1) * LANES
                ]
    ends = edges[...].astype(F32)
    for g in range(SETS):
        sides = [
            jnp.concatenate([ends[:, 4 * g + side, :], ends[:, 4 * g + 2 + side, :]], axis=1)
            for side in range(2)
        ]
        parts = dot(jnp.concatenate(sides, axis=0).astype(BF16), unpack[...])
        for side, column in ((0, 0), (1, WIDTH - 1)):
            for r in range(PACK):
                columns[pl.ds(column * MEMBERS + g * PACK + r, MEM, stride=OWN), :] = parts[
                    side * MEM : (side + 1) * MEM, r * LANES : (r + 1) * LANES
                ]

    for q in range(GROUPS):
        field = columns[q * GROUP * MEMBERS : q * GROUP * MEMBERS + WIDE, :].astype(BF16)
        both = dot(jnp.concatenate(pieces[q], axis=0), field)
        result = both[:WIDE] + both[WIDE:]
        for s in range(GROUP):
            out[pl.ds(q * GROUP + s, MEMBERS, stride=WIDTH), :] = result[
                s * MEMBERS : (s + 1) * MEMBERS
            ]


def exchange_kernel(
    lat_hbm, w_hbm, bias_hbm, cell_hbm, value_hbm, weight_hbm, list_hbm,
    out,
    lat_ref, w_ref, bias_ref, cell_ref, list_ref, blocks, stats, states, edges,
    field, act, wpad, taps, total, halves, turned, turned_rim, cellp, cellc,
    own, edge_out, edge_in, rows_out, ends, ends_out,
    flat, table, picked, placing, stage, columns, diagonal, unpack,
    loaded, edge_sent, edge_got, stat_sent, stat_got, mate_sent, sib_sent, outer_sent, block_got,
    state_sent, state_got, end_sent, end_got,
):
    m = lax.axis_index("mem")
    t = lax.axis_index("lon")
    tiles = lax.axis_size("lon")
    core = lax.rem(t, 2)
    left = lax.rem(t + tiles - 1, tiles)
    right = lax.rem(t + 1, tiles)
    outer = jnp.where(core == 0, left, right)
    inner = jnp.where(core == 0, right, left)
    mine, theirs = 2 * core, 2 - 2 * core
    far = lax.rem(jnp.where(core == 0, t, t + 1), tiles // 2) == 0

    quarter, pair = tiles // 4, lax.rem(t // 2, tiles // 4)
    busy = (pair == 0) | (pair == quarter - 1)

    barrier = pltpu.get_barrier_semaphore()
    for lon in (left, right):
        pl.semaphore_signal(barrier, inc=1, device_id={"lon": lon}, device_id_type=MESH)

    @pl.when(far)
    def _():
        for step in range(1, MEM):
            to = {"mem": lax.rem(m + step, MEM), "lon": outer}
            pl.semaphore_signal(barrier, inc=1, device_id=to, device_id_type=MESH)

    for step in range(1, MEM):
        to = {"mem": lax.rem(m + step, MEM)}
        pl.semaphore_signal(barrier, inc=1, device_id=to, device_id_type=MESH)

    loads = [
        pltpu.make_async_copy(source, target, loaded.at[n])
        for n, (source, target) in enumerate(
            (
                (lat_hbm, lat_ref),
                (w_hbm, w_ref),
                (bias_hbm, bias_ref),
                (cell_hbm, cell_ref),
                (value_hbm, stats.at[1, 0]),
                (weight_hbm, stats.at[1, 1]),
                (list_hbm, list_ref),
            )
        )
    ]
    for load in loads:
        load.start()

    edge_out[...] = jnp.zeros_like(edge_out)
    field[...] = jnp.zeros_like(field)
    wpad[...] = jnp.zeros_like(wpad)
    ends[...] = jnp.zeros_like(ends)
    loads[0].wait()
    for side, column in ((0, WIDTH - 1), (1, 0)):
        edge = lat_ref[:, column].astype(F32).reshape(OWN * LAT, CHANS)
        edge_out[side, :, :CHANS] = edge.astype(BF16)

    for k in range(OWN):
        field[k, LAT : LAT + CELLS, :CHANS] = lat_ref[k].astype(F32).reshape(CELLS, CHANS)
    act[...] = silu(field[...])

    for load in loads[1:-1]:
        load.wait()
    lane = lax.broadcasted_iota(jnp.int32, (LANES, WIDE), 1)
    depth = lax.broadcasted_iota(jnp.int32, (LANES, WIDE), 0)
    blank = jnp.zeros((LANES, LANES), F32)
    for a in range(3):
        for b in range(3):
            wpad[:CHANS, :CHANS] = w_ref[a, b].astype(F32)
            whole = jnp.concatenate([wpad[...], blank], axis=1)
            for r in range(PACK):
                moved = whole if r == 0 else pltpu.roll(whole, CHANS * r, 1)
                taps[r, b * LANES : (b + 1) * LANES, a * WIDE : (a + 1) * WIDE] = moved.astype(BF16)
    for r in range(PACK):
        same = jnp.where((lane - CHANS * r == depth) & (depth < CHANS), 1.0, 0.0)
        taps[r, 3 * LANES :, :WIDE] = jnp.zeros((LANES, WIDE), BF16)
        taps[r, 3 * LANES :, WIDE : 2 * WIDE] = same.astype(BF16)
        taps[r, 3 * LANES :, 2 * WIDE :] = jnp.zeros((LANES, WIDE), BF16)
    wpad[:1, :CHANS] = bias_ref[...]
    bias = jnp.concatenate([wpad[:8, :], blank[:8, :]], axis=1)
    bias = bias + pltpu.roll(bias, CHANS, 1) + pltpu.roll(bias, 2 * CHANS, 1)
    bias = jnp.where(lane[:8, :] < PACK * CHANS, bias, 0.0)[:1, :]

    span = CELLS + LAT
    for g in range(SETS):
        parts = None
        for r in range(PACK):
            k = PACK * g + r
            sides = [act[k, LAT * b : LAT * b + span, :].astype(BF16) for b in range(3)]
            sides.append(field[k, LAT : LAT + span, :].astype(BF16))
            part = dot(jnp.concatenate(sides, axis=1), taps[r])
            parts = part if parts is None else parts + part
        summed = combine(parts) + bias
        total[g, :span] = summed
        total[g, span:] = jnp.zeros((BAND - span, WIDE), F32)
        for h in range(2):
            halves[2 * g + h] = total[g, :, h * LANES : (h + 1) * LANES]

    named = cell_ref[...]
    pixel = jnp.floor((named.astype(F32) + 0.5) * (1.0 / CHANS)).astype(jnp.int32)
    row = jnp.floor((pixel.astype(F32) + 0.5) * (1.0 / WIDTH)).astype(jnp.int32)
    cellc[...] = named - CHANS * pixel
    cellp[...] = (pixel - WIDTH * row) * LAT + row

    pl.semaphore_wait(barrier, jnp.where(far, 2 * MEM, MEM + 1))

    edge_copies = [
        pltpu.make_async_remote_copy(
            src_ref=edge_out.at[side],
            dst_ref=edge_in.at[side],
            send_sem=edge_sent.at[side],
            recv_sem=edge_got.at[side],
            device_id={"lon": lon},
            device_id_type=MESH,
        )
        for side, lon in ((0, right), (1, left))
    ]
    stat_copies = [
        pltpu.make_async_remote_copy(
            src_ref=stats.at[1],
            dst_ref=stats.at[2 * side],
            send_sem=stat_sent.at[side],
            recv_sem=stat_got.at[side],
            device_id={"lon": lon},
            device_id_type=MESH,
        )
        for side, lon in ((0, right), (1, left))
    ]
    for copy in edge_copies:
        copy.start()


    def mend(side):
        pltpu.make_async_remote_copy(
            src_ref=edge_out.at[side],
            dst_ref=edge_in.at[side],
            send_sem=edge_sent.at[side],
            recv_sem=edge_got.at[side],
            device_id={"lon": inner},
            device_id_type=MESH,
        ).wait_recv()
        turn = silu(edge_in[side].astype(F32)).astype(BF16).astype(F32)
        tap = pl.multiple_of(2 * side * LANES, LANES)
        parts = None
        for r in range(PACK):
            pick = [turn[(PACK * g + r) * LAT : (PACK * g + r + 1) * LAT] for g in range(SETS)]
            part = dot(jnp.concatenate(pick, axis=0).astype(BF16), taps[r, pl.ds(tap, LANES)])
            parts = part if parts is None else parts + part
        extra = combine(parts)
        first = pl.multiple_of(side * (CELLS - LAT), LAT)
        for g in range(SETS):
            edge = total[g, pl.ds(first, LAT)] + extra[g * LAT : (g + 1) * LAT]
            total[g, pl.ds(first, LAT)] = edge
            for h in range(2):
                ends[pl.ds(4 * g + 2 * h + side, LAT, stride=16), :] = edge[
                    :, h * LANES : (h + 1) * LANES
                ]

    for i in range(LAT):
        for half in range(2 * SETS):
            rows_out[i, :, half * LANES : (half + 1) * LANES] = halves[
                half, pl.ds(i, SLOT, stride=LAT), :
            ].astype(BF16)
    states[m] = rows_out[m]

    def row_copy(to, source):
        return pltpu.make_async_remote_copy(
            src_ref=rows_out.at[to],
            dst_ref=states.at[source],
            send_sem=state_sent.at[to],
            recv_sem=state_got.at[source],
            device_id={"mem": to},
            device_id_type=MESH,
        )

    def end_copy(to, source):
        return pltpu.make_async_remote_copy(
            src_ref=ends_out.at[to],
            dst_ref=edges.at[source],
            send_sem=end_sent.at[to],
            recv_sem=end_got.at[source],
            device_id={"mem": to},
            device_id_type=MESH,
        )


    @pl.when(busy)
    def _():
        for step in EARLY:
            row_copy(lax.rem(m + step, MEM), m).start()

    build_constants(placing, diagonal, unpack)
    channel = lax.broadcasted_iota(jnp.int32, (WIDE, WIDE), 0)
    rim = pl.multiple_of(jnp.where(core == 0, 0, CELLS - LAT), LAT)

    def choose_from(source, first_cell, more):
        place = lax.broadcasted_iota(jnp.int32, (source.shape[1], LANES), 0) + first_cell

        def choose(pair, carry):
            rows = [pl.ds(2 * pair + n, 1) for n in range(2)]
            hot = jnp.concatenate(
                [jnp.where(place == cellp[at, :], 1.0, 0.0).astype(BF16) for at in rows], axis=1
            )
            chans = jnp.concatenate([cellc[at, :] for at in rows], axis=1)
            for g in range(SETS):
                cells = dot(source[g * WIDE : (g + 1) * WIDE, :], hot)
                for r in range(PACK):
                    low, high = CHANS * r // 8 * 8, -(-CHANS * (r + 1) // 8) * 8
                    mask = channel[low:high] - CHANS * r == chans
                    found = jnp.sum(jnp.where(mask, cells[low:high], 0.0), axis=0, keepdims=True)
                    for n in range(2):
                        spot = pl.ds((PACK * g + r) * 16 + 2 * pair + n, 1)
                        piece = found[:, n * LANES : (n + 1) * LANES]
                        own[spot, :] = own[spot, :] + piece if more else piece
            return carry

        lax.fori_loop(0, OBS // WIDE, choose, 0, unroll=2)

    mend(1 - core)
    cell_row = lax.broadcasted_iota(jnp.int32, (BAND, WIDE), 0)
    for g in range(SETS):
        keep = (cell_row < rim) | (cell_row >= rim + LAT)
        turned[g * WIDE : (g + 1) * WIDE] = jnp.where(keep, total[g], 0.0).T.astype(BF16)
    choose_from(turned, 0, False)

    for copy in stat_copies:
        copy.start()
    mend(core)
    ends_out[...] = ends[...].astype(BF16).reshape(LAT, 16, LANES)
    edges[m] = ends_out[m]
    for g in range(SETS):
        edge = jnp.concatenate(
            [total[g, pl.ds(rim, LAT), :], jnp.zeros((LANES - LAT, WIDE), F32)], axis=0
        )
        turned_rim[g * WIDE : (g + 1) * WIDE] = edge.T.astype(BF16)
    choose_from(turned_rim, rim, True)
    blocks[1, m] = own[...].astype(BF16)

    def arrival(slot, block):
        return pltpu.make_async_remote_copy(
            src_ref=blocks.at[1, block],
            dst_ref=blocks.at[slot, block],
            send_sem=sib_sent.at[block],
            recv_sem=block_got.at[slot, block],
            device_id={"lon": inner},
            device_id_type=MESH,
        )

    def along(block, sent, to):
        return pltpu.make_async_remote_copy(
            src_ref=blocks.at[1, block],
            dst_ref=blocks.at[1, block],
            send_sem=mate_sent.at[sent],
            recv_sem=block_got.at[1, block],
            device_id={"mem": to},
            device_id_type=MESH,
        )

    def across(block):
        return pltpu.make_async_remote_copy(
            src_ref=blocks.at[1, block],
            dst_ref=blocks.at[mine, block],
            send_sem=sib_sent.at[block],
            recv_sem=block_got.at[mine, block],
            device_id={"lon": inner},
            device_id_type=MESH,
        )

    def outward(block, sent, to):
        return pltpu.make_async_remote_copy(
            src_ref=blocks.at[1, block],
            dst_ref=blocks.at[theirs, block],
            send_sem=outer_sent.at[sent],
            recv_sem=block_got.at[theirs, block],
            device_id={"mem": to, "lon": outer},
            device_id_type=MESH,
        )

    half = m // 4 * 4
    partner = lax.rem(m + 4, MEM)
    partner_half = 4 - half
    mates = [half + lax.rem(m + step, 4) for step in range(1, 4)]
    partner_mates = [partner_half + lax.rem(m + step, 4) for step in range(1, 4)]

    along(m, 3, partner).start()

    @pl.when(far)
    def _():
        for step in range(1, MEM, 2):
            to = lax.rem(m + step, MEM)
            outward(m, to, to).start()

    def pass_on(block):
        across(block).start()

        @pl.when(jnp.logical_not(far))
        def _():
            outward(block, block, m).start()

    for n in range(3):
        along(m, n, mates[n]).start()
    pass_on(m)
    for step in range(1, MEM):
        end_copy(lax.rem(m + step, MEM), m).start()
    for n in range(3):
        arrival(1, mates[n]).wait_recv()
        pass_on(mates[n])
    arrival(1, partner).wait_recv()
    for n in range(3):
        along(partner, 4 + n, mates[n]).start()
    pass_on(partner)
    for n in range(3):
        arrival(1, partner_mates[n]).wait_recv()
        pass_on(partner_mates[n])

    @pl.when(jnp.logical_not(busy))
    def _():
        for step in range(1, MEM):
            row_copy(lax.rem(m + step, MEM), m).start()

    beside = m + 1 - 2 * lax.rem(m, 2)

    def hand(block, sent):
        return pltpu.make_async_remote_copy(
            src_ref=blocks.at[mine, block],
            dst_ref=blocks.at[mine, block],
            send_sem=outer_sent.at[sent],
            recv_sem=block_got.at[mine, block],
            device_id={"mem": beside},
            device_id_type=MESH,
        )

    fill(1, blocks, stats, flat, table)

    @pl.when(far)
    def _():
        for step in range(1, MEM, 2):
            block = lax.rem(m + step, MEM)
            arrival(mine, block).wait_recv()
            hand(block, lax.rem(m + step - 1, MEM)).start()

    for copy in stat_copies:
        copy.wait()
    loads[-1].wait()
    for block in range(MEM):
        arrival(theirs, block).wait_recv()
    fill(theirs, blocks, stats, flat, table)
    @pl.when(far)
    def _():
        for step in range(0, MEM, 2):
            arrival(mine, lax.rem(m + step, MEM)).wait_recv()

    @pl.when(jnp.logical_not(far))
    def _():
        for block in range(MEM):
            arrival(mine, block).wait_recv()

    fill(mine, blocks, stats, flat, table)
    def send_late():
        @pl.when(busy)
        def _():
            for step in LATE:
                row_copy(lax.rem(m + step, MEM), m).start()

    pieces = weigh(list_ref, table, picked, placing, stage, diagonal, send_late)

    for step in range(1, MEM):
        other = lax.rem(m + step, MEM)
        row_copy(other, other).wait_recv()
        end_copy(other, other).wait_recv()
    apply(pieces, states, edges, unpack, columns, out)

    for copy in edge_copies:
        copy.wait_send()
    for block in range(MEM):
        across(block).wait_send()
        outward(block, block, m).wait_send()
    along(m, 3, partner).wait_send()
    for n in range(3):
        along(m, n, mates[n]).wait_send()
        along(partner, 4 + n, mates[n]).wait_send()
    for step in range(1, MEM):
        other = lax.rem(m + step, MEM)
        row_copy(other, other).wait_send()
        end_copy(other, other).wait_send()


def exchange(lat, weights, bias, cell, value, weight, lists):
    hbm = pl.BlockSpec(memory_space=pltpu.HBM)
    vmem = pl.BlockSpec(memory_space=pltpu.VMEM)
    dma = pltpu.SemaphoreType.DMA
    return pl.pallas_call(
        exchange_kernel,
        out_shape=jax.ShapeDtypeStruct((MEMBERS * WIDTH, LANES), F32),
        in_specs=[hbm] * 7,
        out_specs=vmem,
        scratch_shapes=[
            pltpu.VMEM(lat.shape, BF16),
            pltpu.VMEM(weights.shape, BF16),
            pltpu.VMEM(bias.shape, F32),
            pltpu.VMEM(cell.shape, jnp.int32),
            pltpu.SMEM(lists.shape, jnp.int32),
            pltpu.VMEM((3, MEM, OWN * 16, LANES), BF16),
            pltpu.VMEM((3, 2, 16, LANES), F32),
            pltpu.VMEM((MEM, SLOT, SETS * WIDE), BF16),
            pltpu.VMEM((MEM, 16, LANES), BF16),
            pltpu.VMEM((OWN, BAND, LANES), F32),
            pltpu.VMEM((OWN, BAND, LANES), F32),
            pltpu.VMEM((LANES, LANES), F32),
            pltpu.VMEM((PACK, 4 * LANES, 3 * WIDE), BF16),
            pltpu.VMEM((SETS, BAND, WIDE), F32),
            pltpu.VMEM((2 * SETS, BAND, LANES), F32),
            pltpu.VMEM((SETS * WIDE, BAND), BF16),
            pltpu.VMEM((SETS * WIDE, LANES), BF16),
            pltpu.VMEM((16, LANES), jnp.int32),
            pltpu.VMEM((16, LANES), jnp.int32),
            pltpu.VMEM((OWN * 16, LANES), F32),
            pltpu.VMEM((2, OWN * LAT, LANES), BF16),
            pltpu.VMEM((2, OWN * LAT, LANES), BF16),
            pltpu.VMEM((LAT, SLOT, SETS * WIDE), BF16),
            pltpu.VMEM((LAT * 16, LANES), F32),
            pltpu.VMEM((LAT, 16, LANES), BF16),
            pltpu.VMEM((MEM * OWN * 16, LANES), F32),
            pltpu.VMEM((3 * OBS, LANES), F32),
            pltpu.VMEM((GROUP, GROUPS * OBS_COL, LANES), F32),
            pltpu.VMEM((GROUP * LANES, 3 * WIDE), BF16),
            pltpu.VMEM((GROUPS * OBS_COL, 3 * WIDE), F32),
            pltpu.VMEM((SLOT * MEMBERS, LANES), F32),
            pltpu.VMEM((WIDE, WIDE), BF16),
            pltpu.VMEM((WIDE, PACK * LANES), BF16),
            dma((7,)),
            dma((2,)),
            dma((2,)),
            dma((2,)),
            dma((2,)),
            dma((7,)),
            dma((MEM,)),
            dma((MEM,)),
            dma((3, MEM)),
            dma((MEM,)),
            dma((MEM,)),
            dma((MEM,)),
            dma((MEM,)),
        ],
        compiler_params=pltpu.CompilerParams(
            collective_id=0, has_side_effects=True, vmem_limit_bytes=60 * 2**20
        ),
    )(lat, weights, bias, cell, value, weight, lists)


def local(latent, conv_weight, conv_bias, obs_cell, obs_value, obs_weight, obs_list):
    result = exchange(
        jnp.transpose(latent, (0, 2, 1, 3)),
        conv_weight,
        conv_bias.reshape(1, CHANS),
        obs_cell.reshape(16, LANES),
        obs_value.reshape(16, LANES),
        obs_weight.reshape(16, LANES),
        obs_list.reshape(WIDTH, 1, OBS_COL),
    )
    return jnp.transpose(result[:, :CHANS].reshape(MEMBERS, WIDTH, 1, CHANS), (0, 2, 1, 3))


def solution(mesh):
    placed = (
        P("mem", None, "lon", None),
        P(),
        P(),
        P("lon"),
        P("lon"),
        P("lon"),
        P("mem", "lon", None),
    )
    return jax.shard_map(
        local, mesh=mesh, in_specs=placed, out_specs=P(None, "mem", "lon", None), check_vma=False
    )
```
